32 devices in a mesh: rows: 4 (over y, x), seq: 8 (over z, core).
Axes of the slice: x: 2, y: 2, z: 4, core: 2. Of those that a mesh axis runs over, the one named last changes fastest.
Arguments:
- inputs: float32 [6, 4, 2048, 512], P(None, 'rows', 'seq'), may hold values from -6 to 6
- starts: int32 [6, 4, 3], P(None, 'rows'), may hold values from 0 to 2047, as said below
- first_gain: float32 [2, 512], replicated, may hold values from 0.1 to 1.9
- conv_taps: float32 [2, 512, 4], replicated, may hold values from -3 to 3
- in_weight: float32 [2, 512, 2048], replicated, may hold values from -0.25 to 0.25
- gate_bias: float32 [2, 1024], replicated, may hold values from -8 to 0
- out_weight: float32 [2, 1024, 512], replicated, may hold values from -0.375 to 0.375
- second_gain: float32 [2, 512], replicated, may hold values from 0.1 to 1.9
- up_weight: float32 [2, 512, 2048], replicated, may hold values from -0.25 to 0.25
- down_weight: float32 [2, 2048, 512], replicated, may hold values from -0.125 to 0.125
- cotangent: float32 [6, 4, 2048, 512], P(None, 'rows', 'seq'), may hold values from -6 to 6
Outputs:
- outputs: float32 [6, 4, 2048, 512], P(None, 'rows', 'seq')
- input_grad: float32 [6, 4, 2048, 512], P(None, 'rows', 'seq')
- first_grad: float32 [2, 512], replicated
- taps_grad: float32 [2, 512, 4], replicated
- in_grad: float32 [2, 512, 2048], P(None, 'seq', 'rows')
- bias_grad: float32 [2, 1024], replicated
- out_grad: float32 [2, 1024, 512], P(None, 'seq', 'rows')
- second_grad: float32 [2, 512], replicated
- up_grad: float32 [2, 512, 2048], P(None, 'seq', 'rows')
- down_grad: float32 [2, 2048, 512], P(None, 'seq', 'rows')
The draws below stay inside these ranges and needn't reach their ends.
Inputs may be any that keep to these rules, and one draw needn't show every extreme that they name: `starts`: each row lists 3 increasing offsets: the first is 0, the second lies in the row's first 256 positions, the third in its last 256 positions.
All inputs are finite; a program needn't handle non-finite values.
Results may differ from the reference program's by a relative error of at most 0.0003.
Values sent between devices are 32-bit elements; how exact they have to be, the bound alone decides.
No kernel may reach another device: no remote copies, remote signals or barrier semaphores. Data moves between devices by JAX's collectives and lax.ppermute only.
A program may use at most 384 MiB of HBM per device.

```python
import jax
import jax.numpy as jnp
from jax import lax

D = 512
H = 1024
FF = 2048
KW = 4
LAYERS = 2
LEN = 2048
NSTART = 3
MICRO = 6
ROWS = 4
GROUP = 256


def draw_starts(key, part):
    key = jax.random.fold_in(key, 11)
    first_key, last_key = jax.random.split(key)
    second = jax.random.randint(first_key, (MICRO, ROWS), 1, GROUP)
    third = jax.random.randint(last_key, (MICRO, ROWS), LEN - GROUP + 1, LEN)
    third = third.at[0, 0].set(LEN - 1)
    return jnp.stack([jnp.zeros_like(second), second, third], -1).astype(jnp.int32)


def level_of(own_key, shape, cuts, smallest, top_value):
    level, own = 1.0, jax.random.fold_in(own_key, 6)
    for position, shards_of in cuts:
        heights = jnp.exp(jax.random.uniform(jax.random.fold_in(own, position), (shards_of,), jnp.float32, smallest / len(cuts), top_value / len(cuts)))
        level = level * jnp.repeat(heights, shape[position] // shards_of).reshape([-1 if axis == position else 1 for axis in range(len(shape))])
    return level


def centred(stream_key, dims, width, most, cuts=(), kind=jnp.bfloat16):
    entries = jax.random.normal(stream_key, dims, jnp.float32) * width
    if len(cuts) > 0:
        entries = level_of(stream_key, dims, cuts, -0.22, 0.18) * entries
    return jnp.clip(entries, min=-most, max=most).astype(kind)


def setup_inputs(seed: int = 0) -> dict:
    arg_keys = jax.random.split(jax.random.key(seed), 12)
    inputs = centred(arg_keys[0], (MICRO, ROWS, LEN, D), 1.0, 6.0, ((1, 4), (2, 8)), jnp.float32)
    starts = draw_starts(jax.random.fold_in(arg_keys[11], 71), 0)
    first_gain = jnp.clip(1.0 + 0.18 * jax.random.normal(arg_keys[2], (LAYERS, D), jnp.float32), 0.1, 1.9)
    conv_taps = centred(arg_keys[3], (LAYERS, D, KW), KW ** -0.5, 3.0, (), jnp.float32)
    in_weight = centred(arg_keys[4], (LAYERS, D, 2 * H), D ** -0.5, 0.25, (), jnp.float32)
    gate_bias = jnp.clip(jax.random.uniform(arg_keys[5], (LAYERS, H), jnp.float32, -8.0, 0.0), -8.0, 0.0)
    out_weight = centred(arg_keys[6], (LAYERS, H, D), (H // 4) ** -0.5, 0.375, (), jnp.float32)
    second_gain = jnp.clip(1.0 + 0.18 * jax.random.normal(arg_keys[7], (LAYERS, D), jnp.float32), 0.1, 1.9)
    up_weight = centred(arg_keys[8], (LAYERS, D, FF), D ** -0.5, 0.25, (), jnp.float32)
    down_weight = centred(arg_keys[9], (LAYERS, FF, D), FF ** -0.5, 0.125, (), jnp.float32)
    cotangent = centred(arg_keys[10], (MICRO, ROWS, LEN, D), 1.0, 6.0, ((1, 4), (2, 8)), jnp.float32)
    return dict(inputs=inputs, starts=starts, first_gain=first_gain, conv_taps=conv_taps, in_weight=in_weight, gate_bias=gate_bias, out_weight=out_weight, second_gain=second_gain, up_weight=up_weight, down_weight=down_weight, cotangent=cotangent)


@jax.custom_vjp
def low(v):
    return lax.optimization_barrier(v.astype(jnp.bfloat16)).astype(jnp.float32)

@jax.custom_vjp
def low_back(v):
    return v

def low_keep(v):
    return (low(v), None)

def low_pass(kept, grad):
    return (grad,)

def back_keep(v):
    return (v, None)

def back_low(kept, grad):
    return (low(grad),)
low.defvjp(low_keep, low_pass)
low_back.defvjp(back_keep, back_low)
epsilon = 1e-05

def rms_scale(values, gain):
    return values * lax.rsqrt(lax.optimization_barrier(jnp.mean(values * values, -1, keepdims=True)) + epsilon) * gain

def combine_pairs(earlier, later):
    return (earlier[0] * later[0], later[0] * earlier[1] + later[1])

def project(left, right):
    return jnp.dot(left, right, precision=lax.Precision.HIGHEST)

def forward_row(row, starts_row, params):
    first_gain, conv_taps, in_weight, gate_bias, out_weight, second_gain, up_weight, down_weight = params
    positions = jnp.arange(1 - KW, LEN, dtype=jnp.int32)
    doc_ext = lax.optimization_barrier(jnp.sum((starts_row[None, :] <= positions[:, None]).astype(jnp.int32), -1))
    own = doc_ext[KW - 1:]
    keep = (own == doc_ext[KW - 2:-1]).astype(row.dtype)[:, None]
    masks = [(doc_ext[KW - 1 - j:KW - 1 - j + LEN] == own).astype(row.dtype)[:, None] for j in range(KW)]
    state_x = row
    for layer in range(LAYERS):
        normed = rms_scale(state_x, first_gain[layer])
        extended = jnp.pad(normed, ((KW - 1, 0), (0, 0)))
        mixed = conv_taps[layer, :, 0] * masks[0] * extended[KW - 1:KW - 1 + LEN]
        for j in range(1, KW):
            mixed = mixed + conv_taps[layer, :, j] * masks[j] * extended[KW - 1 - j:KW - 1 - j + LEN]
        projected = project(mixed, in_weight[layer])
        logit = projected[:, :H] + gate_bias[layer]
        candidate = projected[:, H:]
        decay = jax.nn.sigmoid(-logit) * keep
        drive = jax.nn.sigmoid(logit) * jax.nn.softplus(candidate)
        states = lax.associative_scan(combine_pairs, (decay, drive), axis=0)[1]
        middle = state_x + project(states, out_weight[layer])
        normed2 = rms_scale(middle, second_gain[layer])
        act = jax.nn.gelu(project(normed2, up_weight[layer]), approximate=True)
        state_x = middle + project(act, down_weight[layer])
    return state_x

def reference(inputs, starts, first_gain, conv_taps, in_weight, gate_bias, out_weight, second_gain, up_weight, down_weight, cotangent):
    params = (first_gain, conv_taps, in_weight, gate_bias, out_weight, second_gain, up_weight, down_weight)
    rows_x = inputs.reshape(-1, LEN, D)
    rows_s = starts.reshape(-1, NSTART)
    rows_c = cotangent.reshape(-1, LEN, D)

    def step(total, item):
        row, starts_row, row_cot = item

        def single(values, weights):
            return forward_row(values, starts_row, weights)
        result, back = jax.vjp(single, row, params)
        row_grad, param_grads = back(row_cot)
        total = jax.tree.map(jnp.add, total, param_grads)
        return (total, (result, row_grad))
    zeros = jax.tree.map(jnp.zeros_like, params)
    total, (results, row_grads) = lax.scan(step, zeros, (rows_x, rows_s, rows_c))
    return (results.reshape(inputs.shape), row_grads.reshape(inputs.shape), total[0], total[1], total[2], total[3], total[4], total[5], total[6], total[7])
```

```python
import functools
import math

import jax
import jax.numpy as jnp
from jax import lax
from jax.experimental import pallas as pl
from jax.experimental.pallas import tpu as pltpu
from jax.sharding import PartitionSpec as P

epsilon = 1e-05
C0 = math.sqrt(2.0 / math.pi)
C1 = C0 * 0.044715
NN = (((1,), (0,)), ((), ()))
NT = (((1,), (1,)), ((), ()))
BF = jnp.bfloat16
F32 = jnp.float32
VMEM = 60 * 1024 * 1024
CHUNK = 512
HALF = 256
LARGE = 256 * 1024


def split(v):
    high = v.astype(BF)
    return high, (v - high.astype(F32)).astype(BF)


def dot(left, right, dims=NN):
    return lax.dot_general(left, right, dimension_numbers=dims, preferred_element_type=F32)


def put_right(ref, high, low, axis, at=0):
    size = ref.shape[axis] // 3
    count = high.shape[axis]
    for k, part in enumerate((high, high, low)):
        where = pl.ds(k * size + at, count)
        if axis == 0:
            ref[where, :] = part
        else:
            ref[:, where] = part


def put_left(ref, v, rows):
    high, low = split(v)
    size = ref.shape[1] // 3
    for k, part in enumerate((high, low, high)):
        ref[rows, k * size : (k + 1) * size] = part


def put_left_turned(ref, v, cols):
    size = ref.shape[1] // 3
    for k in range(0, v.shape[1], 128):
        high, low = split(v[:, k : k + 128].T)
        for q, part in enumerate((high, low, high)):
            ref[k : k + 128, pl.ds(q * size + cols, part.shape[1])] = part


def turn_slice(cat_ref, b, size, n, high_ref, low_ref):
    width = cat_ref.shape[1] // 3
    count = high_ref.shape[0]
    rows = slice(b * size, (b + 1) * size)
    for q, ref in enumerate((high_ref, low_ref)):
        part = cat_ref[rows, pl.ds(pl.multiple_of(q * width + n * count, 128), count)]
        ref[:, rows] = part.T


def three_left(high_ref, low_ref):
    return jnp.concatenate([high_ref[...], low_ref[...], high_ref[...]], 1)


def load_rows(ref, b, tmp, put):
    size = ref.shape[1]
    if tmp is not None:
        for k in range(tmp.shape[0]):
            tmp[k] = ref[b, :, 128 * k : 128 * (k + 1)]
    for r in range(0, size, 16):
        if tmp is None:
            put(r, ref[b, r : r + 16, :])
        else:
            groups = [
                jnp.concatenate([tmp[k, pl.ds(i, 8, stride=size // 8), :] for k in range(tmp.shape[0])], 1)
                for i in (r // 8, r // 8 + 1)
            ]
            put(r, jnp.concatenate(groups, 0))


def store_rows(ref, b, values, tmp):
    if tmp is None:
        ref[b] = values
        return
    rows = ref.shape[1] // 8
    for k in range(tmp.shape[0]):
        for i in range(rows):
            tmp[k, pl.ds(i, 8, stride=rows), :] = values[i * 8 : (i + 1) * 8, 128 * k : 128 * (k + 1)]
        ref[b, :, 128 * k : 128 * (k + 1)] = tmp[k]


def inverse_rms(values):
    return lax.rsqrt(jnp.mean(values * values, -1, keepdims=True) + epsilon)


def norm_back(grad, values):
    scale = inverse_rms(values)
    hat = values * scale
    return scale * (grad - hat * jnp.mean(grad * hat, -1, keepdims=True))


def row_sum(values):
    return jnp.sum(values.reshape(-1, 8, values.shape[-1]), 0)


def extend(ref, edge):
    count = edge.shape[0]
    size = ref.shape[0] - 8 * count
    first = lax.broadcasted_iota(jnp.int32, (8, ref.shape[1]), 0) == 0
    for k in range(count):
        rolled = pltpu.roll(ref[size + 8 * k : size + 8 * (k + 1), :], 1, 0)
        ref[8 * k : 8 * (k + 1), :] = jnp.where(first, edge[k : k + 1], rolled)


def convolve(ext_ref, m_ref, b, taps_ref, r, count):
    taps = taps_ref.shape[0]
    mixed = taps_ref[0:1] * ext_ref[r + 8 * (taps - 1) : r + 8 * (taps - 1) + count, :]
    for j in range(1, taps):
        at = r + 8 * (taps - 1 - j)
        mixed = mixed + taps_ref[j : j + 1] * (m_ref[b, r : r + count, j : j + 1] * ext_ref[at : at + count, :])
    return mixed


def chunk_scan(total, local, back):
    row = lax.broadcasted_iota(jnp.int32, local.shape, 0)
    for dist in (1, 2, 4):
        shift = 8 - dist if back else dist
        valid = (row < 8 - dist) if back else (row >= dist)
        moved_l = pltpu.roll(local, shift, 0)
        moved_t = pltpu.roll(total, shift, 0)
        local = jnp.where(valid, total * moved_l + local, local)
        total = jnp.where(valid, total * moved_t, total)
    shift = 7 if back else 1
    valid = (row < 7) if back else (row >= 1)
    return (
        jnp.where(valid, pltpu.roll(local, shift, 0), 0.0),
        jnp.where(valid, pltpu.roll(total, shift, 0), 1.0),
        local,
        total,
    )


def steps_of(body, n, count):
    if count == 1:
        body(True, True)
        return
    pl.when(n == 0)(lambda: body(True, False))
    if count > 2:
        pl.when((n > 0) & (n < count - 1))(lambda: body(False, False))
    pl.when(n == count - 1)(lambda: body(False, True))


def gates_kernel(natural, layer, *refs):
    x_ref, edge_ref, m_ref, gain_ref, taps_ref, wl_ref, wc_ref, bias_ref = refs[:8]
    sg_ref, sp_ref, eq_ref, own_ref, mth_ref, mtl_ref = refs[8:14]
    rest = list(refs[14:])
    xp_ref = rest.pop(0) if natural else None
    cat_ref, right_ref, ext_ref = rest[:3]
    tmp = rest[3] if natural else None
    batch, size, width = x_ref.shape
    step = sg_ref.shape[-1]
    head = 8 * (taps_ref.shape[0] - 1)
    gain = gain_ref[layer : layer + 1]

    @pl.when(pl.program_id(0) == 0)
    def _():
        def prepare(b, _):
            def put(r, x):
                if natural:
                    xp_ref[b, r : r + 16, :] = x
                ext_ref[head + r : head + r + 16, :] = x * inverse_rms(x) * gain

            load_rows(x_ref, b, tmp, put)
            edge = edge_ref[b]
            extend(ext_ref, edge * inverse_rms(edge) * gain)
            for r in range(0, size, 16):
                mixed = convolve(ext_ref, m_ref, b, taps_ref, r, 16)
                put_left(cat_ref, mixed, pl.ds(pl.multiple_of(b * size + r, 16), 16))
            return _

        lax.fori_loop(0, batch, prepare, 0)

    for k, w_ref in enumerate((wl_ref, wc_ref)):
        high, low = split(w_ref[0])
        for q, part in enumerate((high, high, low)):
            right_ref[q * width : (q + 1) * width, k * step : (k + 1) * step] = part
    bias = bias_ref[layer : layer + 1]

    def product(b):
        return dot(cat_ref[b * size : (b + 1) * size, :], right_ref[...])

    ahead = product(0)
    for b in range(batch):
        now = ahead
        if b + 1 < batch:
            ahead = product(b + 1)
        local = jnp.zeros((8, step), F32)
        total = jnp.ones((8, step), F32)
        for r in range(0, size, 8):
            rows = slice(r, r + 8)
            cand = now[rows, step:]
            gate = 1.0 / (1.0 + jnp.exp(-(now[rows, :step] + bias)))
            soft = jnp.maximum(cand, 0.0) + jnp.log1p(jnp.exp(-jnp.abs(cand)))
            sg_ref[b, rows, :] = gate
            sp_ref[b, rows, :] = soft
            decay = (1.0 - gate) * m_ref[b, rows, 1:2]
            local = decay * local + gate * soft
            total = decay * total
        turn_slice(cat_ref, b, size, pl.program_id(0), mth_ref, mtl_ref)
        parts = chunk_scan(total, local, False)
        eq_ref[b, 0:8, :] = parts[0]
        eq_ref[b, 8:16, :] = parts[1]
        own_ref[0, b : b + 1, :] = parts[3][7:8]
        own_ref[1, b : b + 1, :] = parts[2][7:8]


def gelu_parts(pre):
    sq = pre * pre
    tan = jnp.tanh(pre * (C0 + C1 * sq))
    return sq, tan, 0.5 + 0.5 * tan


def ffn_kernel(natural, layer, first_steps, *refs):
    x_ref, m_ref, sg_ref, sp_ref, eq_ref, inc_ref, wo_ref, gain_ref, up_ref, dn_ref = refs[:10]
    y_ref, last_ref, mid_ref, sth_ref, stl_ref, pre_ref, nth_ref, ntl_ref = refs[10:18]
    cat_ref, ro_ref, ru_ref, rd_ref, act_ref = refs[18:23]
    tmp = refs[23] if natural else None
    batch, size, width = x_ref.shape
    n = pl.program_id(0)

    @pl.when(n < first_steps)
    def _():
        high, low = split(wo_ref[0])
        put_right(ro_ref, high, low, 0)
        group = math.gcd(batch, 3)
        for g in range(0, batch, group):
            block = range(g, g + group)
            state = [eq_ref[b, 0:8] + eq_ref[b, 8:16] * inc_ref[b : b + 1] for b in block]
            for r in range(0, size, 16):
                for k, b in enumerate(block):
                    pair = []
                    for rows in (slice(r, r + 8), slice(r + 8, r + 16)):
                        gate = sg_ref[b, rows, :]
                        decay = (1.0 - gate) * m_ref[b, rows, 1:2]
                        state[k] = decay * state[k] + gate * sp_ref[b, rows, :]
                        pair.append(state[k])
                    rows = slice(b * size + r, b * size + r + 16)
                    sth_ref[rows, :], stl_ref[rows, :] = split(jnp.concatenate(pair, 0))
            for b in block:
                rows = slice(b * size, (b + 1) * size)
                left = jnp.concatenate([sth_ref[rows, :], stl_ref[rows, :], sth_ref[rows, :]], 1)
                mid_ref[b] = dot(left, ro_ref[...]) + jnp.where(n == 0, x_ref[b], mid_ref[b])

    @pl.when(n == first_steps)
    def _():
        gain = gain_ref[layer : layer + 1]

        def prepare(b, _):
            for r in range(0, size, 16):
                middle = mid_ref[b, r : r + 16, :]
                y_ref[b, r : r + 16, :] = middle
                rows = pl.ds(pl.multiple_of(b * size + r, 16), 16)
                put_left(cat_ref, middle * inverse_rms(middle) * gain, rows)
            return _

        lax.fori_loop(0, batch, prepare, 0)

    @pl.when(n >= first_steps)
    def _():
        high, low = split(up_ref[0])
        put_right(ru_ref, high, low, 0)
        high, low = split(dn_ref[0])
        put_right(rd_ref, high, low, 0)

        def product(b):
            return dot(cat_ref[b * size : (b + 1) * size, :], ru_ref[...])

        ahead = product(0)
        for b in range(batch):
            now = ahead
            if b + 1 < batch:
                ahead = product(b + 1)
            act = act_ref.at[b % 2]
            for r in range(0, size, 16):
                pre = now[r : r + 16]
                pre_ref[b * size + r : b * size + r + 16, :] = pre
                put_left(act, pre * gelu_parts(pre)[2], slice(r, r + 16))
            turn_slice(cat_ref, b, size, n - first_steps, nth_ref, ntl_ref)
            y_ref[b] += dot(act[...], rd_ref[...])

    @pl.when(n == pl.num_programs(0) - 1)
    def _():
        count = last_ref.shape[1]

        def finish(b, _):
            for k in range(count):
                row = size - 8 * (count - k) + 7
                last_ref[b, k : k + 1, :] = y_ref[b, row : row + 1, :]
            if natural:
                store_rows(y_ref, b, y_ref[b], tmp)
            return _

        lax.fori_loop(0, batch, finish, 0)


def emit(mine, tile, keep_ref, send_ref, plan, half=0):
    kind, depth, lanes, halves = plan
    if kind == "whole":
        keep_ref[half] = tile
        return
    extra = (0,) if halves == 1 else (half, 0)

    def store(core, ref):
        if kind == "plain":
            zs, ks = ref.shape[-4], ref.shape[-3]
            for z in range(zs):
                for k in range(ks):
                    top = (z * 2 + core) * depth
                    ref[extra + (z, k)] = tile[top : top + depth, 128 * k : 128 * (k + 1)]
        else:
            for r in range(ref.shape[0]):
                for z in range(ref.shape[1]):
                    for k in range(ref.shape[2]):
                        left = (z * 2 + core) * lanes + 128 * k
                        ref[r, z, k] = tile[r * depth : (r + 1) * depth, left : left + 128]

    def stores(core):
        store(core, keep_ref)
        store(1 - core, send_ref)

    pl.when(mine == 0)(lambda: stores(0))
    pl.when(mine != 0)(lambda: stores(1))


def three(high_ref, low_ref):
    return jnp.concatenate([high_ref[...], high_ref[...], low_ref[...]], 0)


def ffn_back_kernel(natural, layer, plans, *refs):
    mine_ref, gy_ref, got_ref, last_ref, first_ref, mid_hbm, gain_ref, nth_hbm, ntl_hbm, pre_ref, dn_ref, up_ref = refs[:12]
    gm_ref, sec_ref, dk_ref, ds_ref, uk_ref, us_ref = refs[12:18]
    cat_ref, gyt_ref, ah_ref, al_ref, gh_ref, gl_ref, rd_ref, ru_ref, gn_ref = refs[18:27]
    mid_ref, nth_ref, ntl_ref, sems = refs[27:31]
    tmp = refs[31] if natural else None
    batch, size, width = gy_ref.shape
    n = pl.program_id(0)
    mine = mine_ref[0]
    gain = gain_ref[layer : layer + 1]
    pairs = ((nth_hbm, nth_ref), (ntl_hbm, ntl_ref), (mid_hbm, mid_ref))
    copies = [pltpu.make_async_copy(a, b, sems.at[k]) for k, (a, b) in enumerate(pairs)]

    @pl.when(n == 0)
    def _():
        for copy in copies:
            copy.start()

        def prepare(b, _):
            start = pl.multiple_of(b * size, size)

            def put(r, gy):
                gm_ref[b, r : r + 16, :] = gy

            load_rows(gy_ref, b, tmp, put)
            if not natural:
                count = last_ref.shape[1]
                at = lax.broadcasted_iota(jnp.int32, (8, width), 0) == 7
                delta = norm_back(got_ref[b] * first_ref[layer + 1 : layer + 2], last_ref[b])
                for k in range(count):
                    row = size - 8 * (count - k)
                    gm_ref[b, row : row + 8, :] += jnp.where(at, delta[k : k + 1], 0.0)
            for r in range(0, size, 16):
                put_left(cat_ref, gm_ref[b, r : r + 16, :], pl.ds(pl.multiple_of(start + r, 16), 16))
            put_left_turned(gyt_ref, gm_ref[b], start)
            return _

        lax.fori_loop(0, batch, prepare, 0)
        sec_ref[...] = jnp.zeros_like(sec_ref)
        gn_ref[...] = jnp.zeros_like(gn_ref)

    high, low = split(dn_ref[0])
    put_right(rd_ref, high, low, 1)
    high, low = split(up_ref[0])
    put_right(ru_ref, high, low, 1)

    def product(b):
        return dot(cat_ref[b * size : (b + 1) * size, :], rd_ref[...], NT)

    ahead = product(0)
    for b in range(batch):
        now = ahead
        if b + 1 < batch:
            ahead = product(b + 1)
        for r in range(0, size, 16):
            rows = slice(b * size + r, b * size + r + 16)
            pre = pre_ref[rows, :]
            sq, tan, half = gelu_parts(pre)
            ah_ref[rows, :], al_ref[rows, :] = split(pre * half)
            slope = half + (0.5 * pre) * (1.0 - tan * tan) * (C0 + (3.0 * C1) * sq)
            gh_ref[rows, :], gl_ref[rows, :] = split(now[r : r + 16] * slope)
        rows = slice(b * size, (b + 1) * size)
        left = jnp.concatenate([gh_ref[rows, :], gl_ref[rows, :], gh_ref[rows, :]], 1)
        gn_ref[rows, :] += dot(left, ru_ref[...], NT)
    emit(mine, dot(gyt_ref[...], three(ah_ref, al_ref)), dk_ref, ds_ref, plans[0])

    @pl.when(n == 0)
    def _():
        copies[0].wait()
        copies[1].wait()

    emit(mine, dot(three_left(nth_ref, ntl_ref), three(gh_ref, gl_ref)), uk_ref, us_ref, plans[1])

    @pl.when(n == pl.num_programs(0) - 1)
    def _():
        copies[2].wait()

        def finish(b, _):
            total = sec_ref[...]
            for r in range(0, size, 16):
                gn = gn_ref[pl.ds(pl.multiple_of(b * size + r, 16), 16), :]
                middle = mid_ref[b, r : r + 16, :]
                scale = inverse_rms(middle)
                hat = middle * scale
                total = total + row_sum(gn * hat)
                gg = gn * gain
                mean = jnp.mean(gg * hat, -1, keepdims=True)
                gm_ref[b, r : r + 16, :] = gm_ref[b, r : r + 16, :] + scale * (gg - hat * mean)
            sec_ref[...] = total
            return _

        lax.fori_loop(0, batch, finish, 0)


def out_back_kernel(afters, *refs):
    gm_ref, m_ref, sg_ref, wo_ref, gs_ref, beq_ref, own_ref, gth_ref, gtl_ref, cat_ref, ro_ref = refs[afters:]
    batch, size, width = gm_ref.shape
    step = sg_ref.shape[-1]
    n = pl.program_id(0)

    def prepare(b):
        for r in range(0, size, 16):
            put_left(cat_ref, gm_ref[b, r : r + 16, :], slice(b * size + r, b * size + r + 16))

    def product(b):
        return dot(cat_ref[b * size : (b + 1) * size, :], ro_ref[...], NT)

    def body(first, _):
        if first:
            prepare(0)
        high, low = split(wo_ref[0])
        put_right(ro_ref, high, low, 1)
        ahead = product(0)
        for b in range(batch):
            gs_ref[b] = ahead
            if b + 1 < batch:
                if first:
                    prepare(b + 1)
                ahead = product(b + 1)
            local = jnp.zeros((8, step), F32)
            total = jnp.ones((8, step), F32)
            for i in reversed(range(size // 8)):
                rows = slice(i * 8, (i + 1) * 8)
                decay = (1.0 - sg_ref[b, rows, :]) * m_ref[b, rows, 1:2]
                local = decay * (gs_ref[b, rows, :] + local)
                total = decay * total
            turn_slice(cat_ref, b, size, n, gth_ref, gtl_ref)
            parts = chunk_scan(total, local, True)
            beq_ref[b, 0:8, :] = parts[0]
            beq_ref[b, 8:16, :] = parts[1]
            own_ref[0, b : b + 1, :] = parts[3][0:1]
            own_ref[1, b : b + 1, :] = parts[2][0:1]

    pl.when(n == 0)(lambda: body(True, False))
    pl.when(n != 0)(lambda: body(False, False))


def out_grad_kernel(plan, mine_ref, gth_ref, gtl_ref, sth_ref, stl_ref, ok_ref, os_ref):
    emit(mine_ref[0], dot(three_left(gth_ref, gtl_ref), three(sth_ref, stl_ref)), ok_ref, os_ref, plan)


def gates_back_kernel(plan, afters, *refs):
    refs = refs[afters:]
    mine_ref, gs_ref, sg_ref, sp_ref, sth_ref, stl_ref, m_ref, beq_ref, ret_ref, inc_ref = refs[:10]
    mth_ref, mtl_ref = refs[10:12]
    glh_ref, gll_ref, gch_ref, gcl_ref, bias_ref, ik_ref, is_ref = refs[12:19]
    batch, size, step = sg_ref.shape
    mine = mine_ref[0]
    top = lax.broadcasted_iota(jnp.int32, (8, step), 0) == 0
    bias_sum = jnp.zeros((8, step), F32)
    group = math.gcd(batch, 2)

    def states(b, r):
        rows = slice(b * size + r, b * size + r + 16)
        return sth_ref[rows, :].astype(F32) + stl_ref[rows, :].astype(F32)

    for g in range(0, batch, group):
        block = range(g, g + group)
        carry = [beq_ref[b, 0:8] + beq_ref[b, 8:16] * ret_ref[b : b + 1] for b in block]
        here = [states(b, size - 16) for b in block]
        wrap = [jnp.where(top, inc_ref[b : b + 1], pltpu.roll(here[k][8:], 1, 0)) for k, b in enumerate(block)]
        for r in reversed(range(0, size, 16)):
            for k, b in enumerate(block):
                below = states(b, r - 16) if r else None
                logits, cands = [], []
                for q in (8, 0):
                    rows = slice(r + q, r + q + 8)
                    prev = here[k][:8] if q else (below[8:] if r else wrap[k])
                    gate = sg_ref[b, rows, :]
                    soft = sp_ref[b, rows, :]
                    other = 1.0 - gate
                    adjoint = gs_ref[b, rows, :] + carry[k]
                    through = adjoint * m_ref[b, rows, 1:2]
                    carry[k] = other * through
                    glogit = gate * other * (adjoint * soft - through * prev)
                    bias_sum = bias_sum + glogit
                    logits.insert(0, glogit)
                    cands.insert(0, adjoint * gate * (1.0 - jnp.exp(-soft)))
                here[k] = below
                rows = slice(b * size + r, b * size + r + 16)
                glh_ref[rows, :], gll_ref[rows, :] = split(jnp.concatenate(logits, 0))
                gch_ref[rows, :], gcl_ref[rows, :] = split(jnp.concatenate(cands, 0))
    bias_ref[...] = bias_sum
    right = jnp.concatenate([three(glh_ref, gll_ref), three(gch_ref, gcl_ref)], 1)
    tile = dot(three_left(mth_ref, mtl_ref), right)
    for half in range(2):
        emit(mine, tile[:, half * step : (half + 1) * step], ik_ref, is_ref, plan, half)


def conv_back_kernel(natural, layer, batch, afters, *refs):
    refs = refs[afters:]
    glh_ref, gll_ref, gch_ref, gcl_ref, m_ref, x_ref, edge_ref, gm_ref, taps_ref, gain_ref, w_ref = refs[:11]
    gx_ref, send_ref, s_ref = refs[11:14]
    right_ref, acc_ref, ext_ref, out_ref = refs[14:18]
    tmp = refs[18] if natural else None
    _, size, width = x_ref.shape
    taps = taps_ref.shape[0]
    head = 8 * (taps - 1)
    n = pl.program_id(0)

    def product(slot):
        high = jnp.concatenate([glh_ref[...], gch_ref[...]], 1)
        low = jnp.concatenate([gll_ref[...], gcl_ref[...]], 1)
        acc_ref[slot] = dot(jnp.concatenate([high, low, high], 1), right_ref[...], NT)

    def finish(slot):
        b = n - 1
        last = lax.broadcasted_iota(jnp.int32, (8, width), 0) == 7
        gain = gain_ref[layer : layer + 1]
        scales = []
        for r in range(0, size, 8):
            x = x_ref[0, r : r + 8, :]
            scales.append(inverse_rms(x))
            ext_ref[head + r : head + r + 8, :] = x * scales[-1]
        edge = edge_ref[b]
        extend(ext_ref, edge * inverse_rms(edge))

        def scaled(j, r):
            return taps_ref[j : j + 1] * (m_ref[b, r : r + 8, j : j + 1] * acc_ref[slot, r : r + 8, :])

        sends = [None] * taps
        tails = {}
        for j in range(1, taps):
            for k in range(j):
                piece = scaled(j, 8 * k)
                tails[j, k] = jnp.where(last, 0.0, pltpu.roll(piece, 7, 0))
                sends[j - k] = piece if sends[j - k] is None else sends[j - k] + piece
        for k in range(1, taps):
            send_ref[b, taps - 1 - k : taps - k, :] = sends[k][0:1]
        sums = [s_ref[8 * j : 8 * (j + 1)] for j in range(taps)]
        for r in range(0, size, 8):
            gmixed = acc_ref[slot, r : r + 8, :]
            hat = ext_ref[head + r : head + r + 8, :]
            gn = taps_ref[0:1] * gmixed
            sums[0] = sums[0] + gmixed * hat
            for j in range(1, taps):
                at = head + r - 8 * j
                sums[j] = sums[j] + m_ref[b, r : r + 8, j : j + 1] * gmixed * ext_ref[at : at + 8, :]
                ahead = r + 8 * j
                gn = gn + (scaled(j, ahead) if ahead < size else tails[j, (ahead - size) // 8])
            gg = gn * gain
            mean = jnp.mean(gg * hat, -1, keepdims=True)
            gx = gm_ref[0, r : r + 8, :] + scales[r // 8] * (gg - hat * mean)
            if natural:
                out_ref[r : r + 8, :] = gx
            else:
                gx_ref[0, r : r + 8, :] = gx
        for j in range(taps):
            s_ref[8 * j : 8 * (j + 1)] = sums[j]
        if natural:
            store_rows(gx_ref, 0, out_ref[...], tmp)

    @pl.when(n == 0)
    def _():
        s_ref[...] = jnp.zeros_like(s_ref)
        high, low = split(w_ref[0])
        put_right(right_ref, high, low, 1)
        product(0)

    for odd in range(2):

        @pl.when((n > 0) & (n < batch) & (n % 2 == odd))
        def _():
            product(odd)
            finish(1 - odd)

    @pl.when(n == batch)
    def _():
        finish((batch - 1) % 2)


def add_kernel(count, afters, *refs):
    refs = refs[afters:]
    out_ref = refs[2 * count]
    start = 0
    for k in range(count):
        rows = refs[2 * k].shape[-2]
        out_ref[:, :, start : start + rows, :] = refs[2 * k][...] + refs[2 * k + 1][...]
        start += rows


def shape(*dims, dtype=F32):
    return jax.ShapeDtypeStruct(dims, dtype)


def fixed(array):
    zero = (0,) * len(array.shape)
    return (array, pl.BlockSpec(array.shape, lambda n: zero, pipeline_mode=pl.Buffered(1)))


def in_hbm(array):
    return (array, pl.BlockSpec(memory_space=pltpu.HBM))


def out_fixed(*dims):
    zero = (0,) * len(dims)
    return (shape(*dims), pl.BlockSpec(dims, lambda n: zero))


def chunked(array, at=lambda n: n, axis=-1, layer=None, step=CHUNK):
    dims = list(array.shape)
    axis = axis % len(dims)
    dims[axis] = step
    if layer is not None:
        dims[0] = 1

    def index(n):
        place = [0] * len(dims)
        place[axis] = at(n)
        if layer is not None:
            place[0] = layer
        return tuple(place)

    return (array, pl.BlockSpec(tuple(dims), index))


def block_bytes(dims, dtype):
    dims = [1 if d is None else d for d in dims]
    size = jnp.dtype(dtype).itemsize
    dims[-1] = -(-dims[-1] // 128) * 128
    if len(dims) > 1:
        dims[-2] = -(-dims[-2] // 8) * 8
    return math.prod(dims) * size


def vmem_need(ins, outs, scratch):
    total = 8 * 1024 * 1024
    for array, spec in list(ins) + list(outs):
        if spec.block_shape is not None:
            total += block_bytes(spec.block_shape, array.dtype) * (2 if spec.pipeline_mode is None else 1)
    for ref in scratch:
        if ref.memory_space == pltpu.VMEM:
            total += block_bytes(ref.shape, ref.dtype)
    return min(total, VMEM)


def call(kernel, grid, ins, outs, scratch=(), flops=0, name=None, free=False):
    def large(array):
        return math.prod(array.shape) * array.dtype.itemsize > LARGE

    args = [
        pltpu.with_memory_space_constraint(array, pltpu.HBM)
        if spec.memory_space == pltpu.HBM or (spec.memory_space is None and large(array) and not free)
        else array
        for array, spec in ins
    ]
    shapes = [pltpu.HBM(array.shape, array.dtype) if large(array) and not free else array for array, _ in outs]
    moved = sum(math.prod(a.shape) * a.dtype.itemsize for a, _ in ins)
    moved += sum(math.prod(a.shape) * a.dtype.itemsize for a, _ in outs)
    return pl.pallas_call(
        kernel,
        grid=(grid,),
        in_specs=[s for _, s in ins],
        out_specs=[s for _, s in outs],
        out_shape=shapes,
        scratch_shapes=list(scratch),
        compiler_params=pltpu.CompilerParams(
            vmem_limit_bytes=vmem_need(ins, outs, scratch), dimension_semantics=("arbitrary",)
        ),
        cost_estimate=pl.CostEstimate(flops=int(flops), bytes_accessed=int(moved), transcendentals=0),
        name=name,
    )(*args)


def kept_back(arrays):
    return [in_hbm(a) for a in arrays]


def shift(block, distance):
    size = lax.axis_size("seq")
    route = [(i - distance, i) for i in range(size) if 0 <= i - distance < size]
    return lax.ppermute(block, "seq", route)


def partner(block, flip):
    return lax.ppermute(block, "seq", [(i, i ^ flip) for i in range(lax.axis_size("seq"))])


def combine(earlier, later):
    return jnp.stack([earlier[0] * later[0], later[0] * earlier[1] + later[1]])


def carry_kernel(afters, flag_ref, first_ref, second_ref, out_ref):
    swap = flag_ref[0] == 0
    first, second = first_ref[...], second_ref[...]
    earlier = jnp.where(swap, second, first)
    later = jnp.where(swap, first, second)
    out_ref[0] = earlier[0] * later[0]
    out_ref[1] = later[0] * earlier[1] + later[1]


def joined_carry(first, second, flag, afters):
    def kernel(*refs):
        carry_kernel(0, *refs[len(afters) :])

    flag = (flag.astype(jnp.int32).reshape(1), pl.BlockSpec(memory_space=pltpu.SMEM))
    return call(
        kernel,
        1,
        kept_back(afters) + [flag, fixed(first), fixed(second)],
        [out_fixed(*first.shape)],
        name="carry",
    )[0]


def incoming_carry(own, back, fillers=((), ())):
    size = lax.axis_size("seq")
    other = partner(own, 1)
    odd = lax.axis_index("seq") % 2 == 1
    is_later = ~odd if back else odd
    if back:
        pair = joined_carry(other, own, is_later, fillers[0])
    else:
        pair = jnp.where(is_later, combine(other, own), combine(own, other))
    sign = -2 if back else 2
    before = None
    dist = 1
    while dist < size // 2:
        got = shift(pair, sign * dist)
        before = got if before is None else combine(got, before)
        if 2 * dist < size // 2:
            if back and dist == 1:
                pair = joined_carry(got, pair, jnp.ones((), jnp.int32), fillers[1])
            else:
                pair = combine(got, pair)
        dist *= 2
    enters = jnp.where(is_later, other[0] * before[1] + other[1], before[1])
    return (enters, pair) if back else enters


def document_masks(starts_rows, group):
    place = jnp.arange(group, dtype=jnp.int32)
    position = lax.axis_index("seq") * group + (place % 8) * (group // 8) + place // 8
    back = position[:, None] - jnp.arange(8, dtype=jnp.int32)

    def document(at):
        return sum((starts_rows[:, k, None, None] <= at).astype(jnp.int32) for k in range(starts_rows.shape[1]))

    return (document(back) == document(position[:, None])).astype(F32)


class Grad:
    def __init__(self, height, width, flip, direct, step, halves=1):
        self.rows = lax.axis_size("rows")
        self.seq = lax.axis_size("seq")
        self.flip = flip
        self.direct = direct
        self.height = height
        self.width = width
        self.depth = height // (self.rows if flip else self.seq)
        self.lanes = width * halves // (self.seq if flip else self.rows)
        zs = self.seq // 2
        if not direct:
            self.plan = ("whole", 0, 0, halves)
            self.out = (shape(halves, height, width), pl.BlockSpec((halves, height, step), lambda n: (0, 0, n)))
        elif flip:
            self.plan = ("flip", self.depth, self.lanes, 1)
            ks = self.lanes // 128
            dims = (self.rows, zs, ks, self.depth, 128)
            block = (self.rows, step // (2 * self.lanes), ks, self.depth, 128)
            self.out = (shape(*dims), pl.BlockSpec(block, lambda n: (0, n, 0, 0, 0)))
        else:
            self.plan = ("plain", self.depth, self.lanes, halves)
            per = self.lanes // step
            dims = (self.rows // halves, zs, self.lanes // 128, self.depth, 128)
            block = (1, zs, step // 128, self.depth, 128)
            if halves == 1:
                self.out = (shape(*dims), pl.BlockSpec(block, lambda n: (n // per, 0, n % per, 0, 0)))
            else:
                spec = pl.BlockSpec((halves,) + block, lambda n: (0, n // per, 0, n % per, 0, 0))
                self.out = (shape(halves, *dims), spec)

    def outs(self):
        return [self.out, self.out if self.direct else out_fixed(8, 128)]

    def pieces(self, array):
        return array.reshape(self.rows, self.seq // 2, -1, 128)

    def whole(self, array):
        out = array.reshape(self.lanes // 128, self.depth, 128).swapaxes(0, 1).reshape(self.depth, self.lanes)
        return out.T if self.flip else out

    def plain_sum(self, value):
        value = jnp.concatenate(list(value), 1)
        value = lax.psum_scatter(value, "seq", scatter_dimension=1 if self.flip else 0, tiled=True)
        value = lax.psum_scatter(value, "rows", scatter_dimension=0 if self.flip else 1, tiled=True)
        return value.T if self.flip else value


def butterfly(value):
    for axis in ("seq", "rows"):
        size = lax.axis_size(axis)
        flip = 1
        while flip < size:
            value = value + lax.ppermute(value, axis, [(i, i ^ flip) for i in range(size)])
            flip *= 2
    return value


def pair_sum(parts, afters=()):
    ins = []
    for kept, sent in parts:
        got = partner(sent, 1)
        ins += [kept, got]
    count = len(parts)
    rows, zs = ins[0].shape[:2]
    total = sum(a.shape[2] for a in ins[::2])
    return call(
        functools.partial(add_kernel, count, len(afters)),
        rows,
        kept_back(afters)
        + [(a, pl.BlockSpec((1,) + a.shape[1:], lambda n: (n, 0, 0, 0))) for a in ins],
        [(shape(rows, zs, total, 128), pl.BlockSpec((1, zs, total, 128), lambda n: (n, 0, 0, 0)))],
        name="neighbour_sum",
        free=True,
    )[0]


def reduce_rows(pieces):
    return lax.psum_scatter(pieces, "rows", scatter_dimension=0, tiled=True)[0]


def seq_step(arrays, dist, got=None, afters=()):
    count = len(arrays)
    places = arrays[0].shape[0]
    total = sum(a.shape[1] for a in arrays)
    bit = ((lax.axis_index("seq") // 2 // dist) % 2).astype(jnp.int32).reshape(1)

    def kernel(*refs):
        refs = refs[len(afters) :]
        own = refs[0][0]
        ins = refs[1 : 1 + count]
        more = refs[1 + count] if got is not None else None
        outs = refs[1 + count + (got is not None) :]
        start = 0
        for ref in ins:
            rows = ref.shape[1]
            for z in range(places):
                value = ref[z]
                if more is not None:
                    value = value + more[z, start : start + rows, :]
                if places == 1:
                    outs[0][0, start : start + rows, :] = value
                    continue

                def put(ref, value=value, start=start, rows=rows, z=z):
                    ref[z // 2, start : start + rows, :] = value

                pl.when(own == z % 2)(functools.partial(put, outs[0]))
                pl.when(own != z % 2)(functools.partial(put, outs[1]))
            start += rows

    half = max(1, places // 2)
    return call(
        kernel,
        1,
        kept_back(afters)
        + [(bit, pl.BlockSpec(memory_space=pltpu.SMEM))]
        + [fixed(a) for a in arrays]
        + ([fixed(got)] if got is not None else []),
        [out_fixed(half, total, 128) for _ in range(2 if places > 1 else 1)],
        name="seq_sum",
        free=True,
    )


def reduce_seq(kept, afters=()):
    dist = 1
    while len(kept) == 2:
        got = partner(kept[1], 2 * dist)
        dist *= 2
        kept = seq_step([kept[0]], dist, got, afters)
    return kept[0][0]


def per_device(
    inputs,
    starts,
    first_gain,
    conv_taps,
    in_weight,
    gate_bias,
    out_weight,
    second_gain,
    up_weight,
    down_weight,
    cotangent,
):
    dims = inputs.shape
    batch = dims[0] * dims[1]
    group = dims[2]
    width = dims[3]
    tokens = batch * group
    taps = conv_taps.shape[2]
    layers = in_weight.shape[0]
    hidden = out_weight.shape[1]
    ff = up_weight.shape[2]
    rows_size, seq_size = lax.axis_size("rows"), lax.axis_size("seq")
    direct = (
        ff % (CHUNK * rows_size) == 0
        and (2 * hidden) % (HALF * rows_size) == 0
        and rows_size % 2 == 0
        and all(n % (128 * seq_size) == 0 and CHUNK % (2 * n // seq_size) == 0 for n in (ff, hidden))
    )
    extended = pltpu.VMEM((8 * (taps - 1) + group, width), F32)
    order = [pltpu.VMEM((width // 128, group, 128), F32)]
    mine = (lax.axis_index("seq") % 2).astype(jnp.int32).reshape(1)
    mine = (mine, pl.BlockSpec(memory_space=pltpu.SMEM))
    masks = document_masks(starts.reshape(batch, -1), group)
    taps_rows = conv_taps.swapaxes(1, 2)
    in_flops = 6 * tokens * width * 2 * hidden
    out_flops = 6 * tokens * width * hidden
    ffn_flops = 6 * tokens * width * ff * 2

    current = inputs.reshape(batch, group, width)
    last_rows = current[:, group - taps + 1 :]
    row_hidden = shape(batch, group, hidden)
    row_eq = shape(batch, 16, hidden)
    row_own = shape(2, batch, hidden)
    turned = shape(width, tokens, dtype=BF)
    saved = []
    for layer in range(layers):
        natural = layer == 0
        final = layer == layers - 1
        edge = shift(last_rows, 1)
        steps = hidden // CHUNK
        res = call(
            functools.partial(gates_kernel, natural, layer),
            steps,
            [fixed(current), fixed(edge), fixed(masks), fixed(first_gain), fixed(taps_rows[layer])]
            + [chunked(in_weight, layer=layer), chunked(in_weight, lambda n: n + steps, layer=layer)]
            + [chunked(gate_bias)],
            [chunked(row_hidden), chunked(row_hidden), chunked(row_eq), chunked(row_own)]
            + [chunked(turned, axis=0, step=width // steps) for _ in range(2)]
            + ([out_fixed(batch, group, width)] if natural else []),
            scratch=[pltpu.VMEM((tokens, 3 * width), BF), pltpu.VMEM((3 * width, 2 * CHUNK), BF), extended]
            + (order if natural else []),
            flops=in_flops,
            name="gates",
        )
        sg, sp, eq, own = res[:4]
        mixt = res[4:6]
        x = res[6] if natural else current
        inc = incoming_carry(own, False)
        early_steps = hidden // HALF

        def early(n):
            return jnp.minimum(n, early_steps - 1)

        def late(n):
            return jnp.maximum(n - early_steps, 0)

        def halves(array):
            return chunked(array, early, step=HALF)

        res = call(
            functools.partial(ffn_kernel, final, layer, early_steps),
            early_steps + ff // CHUNK,
            [fixed(x), fixed(masks), halves(sg), halves(sp), halves(eq), halves(inc)]
            + [chunked(out_weight, early, axis=1, layer=layer, step=HALF), fixed(second_gain)]
            + [chunked(up_weight, late, layer=layer), chunked(down_weight, late, axis=1, layer=layer)],
            [
                out_fixed(batch, group, width),
                out_fixed(batch, taps - 1, width),
                out_fixed(batch, group, width),
                halves(shape(tokens, hidden, dtype=BF)),
                halves(shape(tokens, hidden, dtype=BF)),
                chunked(shape(tokens, ff), late),
                chunked(turned, late, axis=0, step=width // (ff // CHUNK)),
                chunked(turned, late, axis=0, step=width // (ff // CHUNK)),
            ],
            scratch=[
                pltpu.VMEM((tokens, 3 * width), BF),
                pltpu.VMEM((3 * HALF, width), BF),
                pltpu.VMEM((3 * width, CHUNK), BF),
                pltpu.VMEM((3 * CHUNK, width), BF),
                pltpu.VMEM((2, group, 3 * CHUNK), BF),
            ]
            + (order if final else []),
            flops=out_flops + ffn_flops,
            name="ffn",
        )
        current, following, mid, st, pre, nt = res[0], res[1], res[2], res[3:5], res[5], res[6:8]
        saved.append((x, last_rows, edge, sg, sp, inc, mid, st, pre, mixt, nt))
        last_rows = following
    outputs = current

    grad = cotangent.reshape(batch, group, width)
    got = jnp.zeros((batch, taps - 1, width), F32)
    down_plan = Grad(width, ff, True, direct, CHUNK)
    up_plan = Grad(width, ff, False, direct, CHUNK)
    out_plan = Grad(width, hidden, True, direct, CHUNK)
    in_plan = Grad(width, hidden, False, direct, HALF, 2)
    shards = [None] * layers
    smalls = [None] * layers
    early_rows = [None] * layers
    late_rows = [None] * layers
    for layer in reversed(range(layers)):
        x, last_rows, edge, sg, sp, inc, mid, st, pre, mixt, nt = saved[layer]
        final = layer == layers - 1
        first = layer == 0
        above = last_rows if final else saved[layer + 1][1]
        res = call(
            functools.partial(ffn_back_kernel, final, layer, (down_plan.plan, up_plan.plan)),
            ff // CHUNK,
            [mine, fixed(grad), fixed(got), fixed(above), fixed(first_gain)]
            + [in_hbm(mid), fixed(second_gain), in_hbm(nt[0]), in_hbm(nt[1]), chunked(pre)]
            + [chunked(down_weight, axis=1, layer=layer), chunked(up_weight, layer=layer)],
            [out_fixed(batch, group, width), out_fixed(8, width)] + down_plan.outs() + up_plan.outs(),
            scratch=[
                pltpu.VMEM((tokens, 3 * width), BF),
                pltpu.VMEM((width, 3 * tokens), BF),
                pltpu.VMEM((tokens, CHUNK), BF),
                pltpu.VMEM((tokens, CHUNK), BF),
                pltpu.VMEM((tokens, CHUNK), BF),
                pltpu.VMEM((tokens, CHUNK), BF),
                pltpu.VMEM((CHUNK, 3 * width), BF),
                pltpu.VMEM((width, 3 * CHUNK), BF),
                pltpu.VMEM((tokens, width), F32),
                pltpu.VMEM((batch, group, width), F32),
                pltpu.VMEM((width, tokens), BF),
                pltpu.VMEM((width, tokens), BF),
                pltpu.SemaphoreType.DMA((3,)),
            ]
            + (order if final else []),
            flops=2 * ffn_flops,
            name="ffn_back",
        )
        gm, sec, down_g, up_g = res[0], res[1], res[2:4], res[4:6]
        waiting = []
        z_next = None
        if direct and not final:
            z_next = seq_step([early_rows[layer + 1], late_rows[layer + 1]], 1, None, [gm])
            waiting = [z_next[1]]
        res = call(
            functools.partial(out_back_kernel, len(waiting)),
            hidden // CHUNK,
            kept_back(waiting) + [fixed(gm), fixed(masks), chunked(sg), chunked(out_weight, axis=1, layer=layer)],
            [chunked(row_hidden), chunked(row_eq), chunked(row_own)]
            + [chunked(turned, axis=0, step=width // (hidden // CHUNK)) for _ in range(2)],
            scratch=[pltpu.VMEM((tokens, 3 * width), BF), pltpu.VMEM((CHUNK, 3 * width), BF)],
            flops=out_flops,
            name="out_back",
        )
        gs, beq, own, gmt = res[0], res[1], res[2], res[3:5]
        out_g = call(
            functools.partial(out_grad_kernel, out_plan.plan),
            hidden // CHUNK,
            [mine, fixed(gmt[0]), fixed(gmt[1]), chunked(st[0]), chunked(st[1])],
            out_plan.outs(),
            flops=out_flops,
            name="out_grad",
        )
        waiting = []
        fillers = [[], list(out_g)]
        if direct:
            early_parts = [tuple(down_plan.pieces(v) for v in down_g), tuple(up_plan.pieces(v) for v in up_g)]
            if first:
                early = pair_sum(early_parts, [gs])
                early_rows[layer] = reduce_rows(early)
                fillers[0].append(early)
        ret, last_pair = incoming_carry(own, True, fillers)
        if direct and not first:
            early = pair_sum(early_parts, [last_pair])
            early_rows[layer] = reduce_rows(early)
            waiting.append(early)
        if z_next is not None:
            z_next = seq_step([z_next[0]], 2, partner(z_next[1], 2), [last_pair])
            waiting.append(z_next[-1])
        steps = hidden // HALF
        halves = functools.partial(chunked, step=HALF)
        res = call(
            functools.partial(gates_back_kernel, in_plan.plan, len(waiting)),
            steps,
            kept_back(waiting)
            + [mine, halves(gs), halves(sg), halves(sp), halves(st[0]), halves(st[1]), fixed(masks)]
            + [halves(beq), halves(ret), halves(inc)]
            + [fixed(mixt[0]), fixed(mixt[1])],
            [halves(shape(tokens, hidden, dtype=BF)) for _ in range(4)] + [halves(shape(8, hidden))] + in_plan.outs(),
            flops=in_flops,
            name="gates_back",
        )
        gproj, bias_sum, in_g = res[:4], res[4], res[5:7]
        waiting = []
        late_parts = None
        if direct:
            late_parts = [tuple(out_plan.pieces(v) for v in out_g), tuple(in_plan.pieces(v) for v in in_g)]
            if first:
                halved = seq_step([early_rows[layer]], 1, None, [bias_sum])
                late = pair_sum(late_parts, [halved[-1]])
                late_rows[layer] = reduce_rows(late)
                waiting = [late]

        def now(n):
            return jnp.minimum(n, batch - 1)

        def lag(n):
            return jnp.maximum(n - 1, 0)

        res = call(
            functools.partial(conv_back_kernel, first, layer, batch, len(waiting)),
            batch + 1,
            kept_back(waiting)
            + [chunked(g, now, axis=0, step=group) for g in gproj]
            + [fixed(masks), chunked(x, lag, axis=0, step=1), fixed(edge), chunked(gm, lag, axis=0, step=1)]
            + [fixed(taps_rows[layer]), fixed(first_gain)]
            + [(in_weight, pl.BlockSpec((1, width, 2 * hidden), lambda n: (layer, 0, 0), pipeline_mode=pl.Buffered(1)))],
            [
                chunked(shape(batch, group, width), lag, axis=0, step=1),
                out_fixed(batch, taps - 1, width),
                out_fixed(8 * taps, width),
            ],
            scratch=[pltpu.VMEM((width, 6 * hidden), BF), pltpu.VMEM((2, group, width), F32)]
            + [extended, pltpu.VMEM((group, width), F32)]
            + (order if first else []),
            flops=in_flops,
            name="conv_back",
        )
        grad, send, sums = res
        if z_next is not None:
            dist = 2
            while len(z_next) == 2:
                got = partner(z_next[1], 2 * dist)
                dist *= 2
                z_next = seq_step([z_next[0]], dist, got, [grad])
            early_rows[layer + 1] = z_next[0][0]
        if direct and not first:
            late_rows[layer] = reduce_rows(pair_sum(late_parts, [grad]))
        if not direct:
            shards[layer] = (
                in_plan.plain_sum(in_g[0]),
                out_plan.plain_sum(out_g[0]),
                up_plan.plain_sum(up_g[0]),
                down_plan.plain_sum(down_g[0]),
            )
        got = shift(send, -1)
        if first:
            grad = grad.at[:, group - taps + 1 :].add(norm_back(got * first_gain[layer], last_rows))
        smalls[layer] = jnp.concatenate(
            [
                jnp.sum(sums.reshape(taps, 8, width), 1),
                jnp.sum(sec, 0, keepdims=True),
                jnp.sum(bias_sum, 0).reshape(-1, width),
            ],
            0,
        )

    if direct:
        down_k = down_plan.depth * down_plan.lanes // 128
        up_k = up_plan.depth * up_plan.lanes // 128
        out_k = out_plan.depth * out_plan.lanes // 128
        done = early_rows[1:]
        early = reduce_seq(halved, [sums])
        late = reduce_seq(seq_step([late_rows[0]], 1))
        done.insert(0, jnp.concatenate([early, late], 0))
        for layer in range(layers):
            parts = jnp.split(done[layer], [down_k, down_k + up_k, down_k + up_k + out_k])
            plans = (down_plan, up_plan, out_plan, in_plan)
            shards[layer] = tuple(plan.whole(part) for plan, part in zip(plans, parts))[::-1]
    in_grad, out_grad, up_grad, down_grad = (jnp.stack([s[k] for s in shards]) for k in range(4))
    every = butterfly(jnp.stack(smalls))
    sums = every[:, :taps]
    first_grad = jnp.sum(sums * taps_rows, 1)
    taps_grad = (sums * first_gain[:, None]).swapaxes(1, 2)
    second_grad = every[:, taps]
    bias_grad = every[:, taps + 1 :].reshape(layers, hidden)
    return (
        outputs.reshape(dims),
        grad.reshape(dims),
        first_grad,
        taps_grad,
        in_grad,
        bias_grad,
        out_grad,
        second_grad,
        up_grad,
        down_grad,
    )


def solution(mesh):
    in_specs = (
        P(None, "rows", "seq", None),
        P(None, "rows", None),
        P(),
        P(),
        P(),
        P(),
        P(),
        P(),
        P(),
        P(),
        P(None, "rows", "seq", None),
    )
    out_specs = (
        P(None, "rows", "seq", None),
        P(None, "rows", "seq", None),
        P(),
        P(),
        P(None, "seq", "rows"),
        P(),
        P(None, "seq", "rows"),
        P(),
        P(None, "seq", "rows"),
        P(None, "seq", "rows"),
    )
    return jax.shard_map(
        per_device, mesh=mesh, in_specs=in_specs, out_specs=out_specs, check_vma=False
    )
```

```python
import functools
import math

import jax
import jax.numpy as jnp
from jax import lax
from jax.experimental import pallas as pl
from jax.experimental.pallas import tpu as pltpu
from jax.sharding import PartitionSpec as P

epsilon = 1e-05
C0 = math.sqrt(2.0 / math.pi)
C1 = C0 * 0.044715
NN = (((1,), (0,)), ((), ()))
NT = (((1,), (1,)), ((), ()))
BF = jnp.bfloat16
F32 = jnp.float32
VMEM = 60 * 1024 * 1024
CHUNK = 512
HALF = 256
LARGE = 256 * 1024


def split(v):
    high = v.astype(BF)
    return high, (v - high.astype(F32)).astype(BF)


def dot(left, right, dims=NN):
    return lax.dot_general(left, right, dimension_numbers=dims, preferred_element_type=F32)


def put_right(ref, high, low, axis, at=0):
    size = ref.shape[axis] // 3
    count = high.shape[axis]
    for k, part in enumerate((high, high, low)):
        where = pl.ds(k * size + at, count)
        if axis == 0:
            ref[where, :] = part
        else:
            ref[:, where] = part


def put_left(ref, v, rows):
    high, low = split(v)
    size = ref.shape[1] // 3
    for k, part in enumerate((high, low, high)):
        ref[rows, k * size : (k + 1) * size] = part


def put_left_turned(ref, v, cols):
    size = ref.shape[1] // 3
    for k in range(0, v.shape[1], 128):
        high, low = split(v[:, k : k + 128].T)
        for q, part in enumerate((high, low, high)):
            ref[k : k + 128, pl.ds(q * size + cols, part.shape[1])] = part


def turn_slice(cat_ref, b, size, n, high_ref, low_ref):
    width = cat_ref.shape[1] // 3
    count = high_ref.shape[0]
    rows = slice(b * size, (b + 1) * size)
    for q, ref in enumerate((high_ref, low_ref)):
        part = cat_ref[rows, pl.ds(pl.multiple_of(q * width + n * count, 128), count)]
        ref[:, rows] = part.T


def three_left(high_ref, low_ref):
    return jnp.concatenate([high_ref[...], low_ref[...], high_ref[...]], 1)


def turn_eight(values):
    row = lax.broadcasted_iota(jnp.int32, values[0].shape, 0)
    for d in (4, 2, 1):
        low = (row & d) == 0
        out = list(values)
        for a in range(8):
            if a & d == 0:
                first, second = values[a], values[a + d]
                out[a] = jnp.where(low, first, pltpu.roll(second, d, 0))
                out[a + d] = jnp.where(low, pltpu.roll(first, 8 - d, 0), second)
        values = out
    return values


def load_rows(ref, b, natural, put):
    size = ref.shape[1]
    if not natural:
        for r in range(0, size, 8):
            put(r, ref[b, r : r + 8, :])
        return
    long = size // 8
    for m in range(0, long, 8):
        for i, value in enumerate(turn_eight([ref[b, c * long + m : c * long + m + 8, :] for c in range(8)])):
            put(8 * (m + i), value)


def store_rows(ref, b, get):
    long = ref.shape[1] // 8
    for m in range(0, long, 8):
        for c, value in enumerate(turn_eight([get(8 * (m + i)) for i in range(8)])):
            ref[b, c * long + m : c * long + m + 8, :] = value


def inverse_rms(values):
    return lax.rsqrt(jnp.mean(values * values, -1, keepdims=True) + epsilon)


def norm_back(grad, values):
    scale = inverse_rms(values)
    hat = values * scale
    return scale * (grad - hat * jnp.mean(grad * hat, -1, keepdims=True))


def row_sum(values):
    return jnp.sum(values.reshape(-1, 8, values.shape[-1]), 0)


def extend(ref, edge):
    count = edge.shape[0]
    size = ref.shape[0] - 8 * count
    first = lax.broadcasted_iota(jnp.int32, (8, ref.shape[1]), 0) == 0
    for k in range(count):
        rolled = pltpu.roll(ref[size + 8 * k : size + 8 * (k + 1), :], 1, 0)
        ref[8 * k : 8 * (k + 1), :] = jnp.where(first, edge[k : k + 1], rolled)


def convolve(ext_ref, m_ref, b, taps_ref, r, count):
    taps = taps_ref.shape[0]
    mixed = taps_ref[0:1] * ext_ref[r + 8 * (taps - 1) : r + 8 * (taps - 1) + count, :]
    for j in range(1, taps):
        at = r + 8 * (taps - 1 - j)
        mixed = mixed + taps_ref[j : j + 1] * (m_ref[b, r : r + count, j : j + 1] * ext_ref[at : at + count, :])
    return mixed


def chunk_scan(total, local, back):
    row = lax.broadcasted_iota(jnp.int32, local.shape, 0)
    for dist in (1, 2, 4):
        shift = 8 - dist if back else dist
        valid = (row < 8 - dist) if back else (row >= dist)
        moved_l = pltpu.roll(local, shift, 0)
        moved_t = pltpu.roll(total, shift, 0)
        local = jnp.where(valid, total * moved_l + local, local)
        total = jnp.where(valid, total * moved_t, total)
    shift = 7 if back else 1
    valid = (row < 7) if back else (row >= 1)
    return (
        jnp.where(valid, pltpu.roll(local, shift, 0), 0.0),
        jnp.where(valid, pltpu.roll(total, shift, 0), 1.0),
        local,
        total,
    )


def steps_of(body, n, count):
    if count == 1:
        body(True, True)
        return
    pl.when(n == 0)(lambda: body(True, False))
    if count > 2:
        pl.when((n > 0) & (n < count - 1))(lambda: body(False, False))
    pl.when(n == count - 1)(lambda: body(False, True))


def gates_kernel(natural, layer, *refs):
    x_ref, edge_ref, m_ref, gain_ref, taps_ref, wl_ref, wc_ref, bias_ref = refs[:8]
    sg_ref, sp_ref, eq_ref, own_ref, mth_ref, mtl_ref = refs[8:14]
    rest = list(refs[14:])
    xp_ref = rest.pop(0) if natural else None
    cat_ref, right_ref, ext_ref = rest[:3]
    batch, size, width = x_ref.shape
    step = sg_ref.shape[-1]
    head = 8 * (taps_ref.shape[0] - 1)
    gain = gain_ref[layer : layer + 1]

    @pl.when(pl.program_id(0) == 0)
    def _():
        def prepare(b, _):
            def put(r, x):
                if natural:
                    xp_ref[b, r : r + 8, :] = x
                ext_ref[head + r : head + r + 8, :] = x * inverse_rms(x) * gain

            load_rows(x_ref, b, natural, put)
            edge = edge_ref[b]
            extend(ext_ref, edge * inverse_rms(edge) * gain)
            for r in range(0, size, 16):
                mixed = convolve(ext_ref, m_ref, b, taps_ref, r, 16)
                put_left(cat_ref, mixed, pl.ds(pl.multiple_of(b * size + r, 16), 16))
            return _

        lax.fori_loop(0, batch, prepare, 0)

    for k, w_ref in enumerate((wl_ref, wc_ref)):
        high, low = split(w_ref[0])
        for q, part in enumerate((high, high, low)):
            right_ref[q * width : (q + 1) * width, k * step : (k + 1) * step] = part
    bias = bias_ref[layer : layer + 1]

    def product(b):
        return dot(cat_ref[b * size : (b + 1) * size, :], right_ref[...])

    ahead = product(0)
    for b in range(batch):
        now = ahead
        if b + 1 < batch:
            ahead = product(b + 1)
        local = jnp.zeros((8, step), F32)
        total = jnp.ones((8, step), F32)
        for r in range(0, size, 8):
            rows = slice(r, r + 8)
            cand = now[rows, step:]
            gate = 1.0 / (1.0 + jnp.exp(-(now[rows, :step] + bias)))
            soft = jnp.maximum(cand, 0.0) + jnp.log1p(jnp.exp(-jnp.abs(cand)))
            sg_ref[b, rows, :] = gate
            sp_ref[b, rows, :] = soft
            decay = (1.0 - gate) * m_ref[b, rows, 1:2]
            local = decay * local + gate * soft
            total = decay * total
        turn_slice(cat_ref, b, size, pl.program_id(0), mth_ref, mtl_ref)
        parts = chunk_scan(total, local, False)
        eq_ref[b, 0:8, :] = parts[0]
        eq_ref[b, 8:16, :] = parts[1]
        own_ref[0, b : b + 1, :] = parts[3][7:8]
        own_ref[1, b : b + 1, :] = parts[2][7:8]


def gelu_parts(pre):
    sq = pre * pre
    tan = jnp.tanh(pre * (C0 + C1 * sq))
    return sq, tan, 0.5 + 0.5 * tan


def ffn_kernel(natural, layer, first_steps, *refs):
    x_ref, m_ref, sg_ref, sp_ref, eq_ref, inc_ref, wo_ref, gain_ref, up_ref, dn_ref = refs[:10]
    y_ref, last_ref, mid_ref, sth_ref, stl_ref, pre_ref, nth_ref, ntl_ref = refs[10:18]
    cat_ref, ro_ref, ru_ref, rd_ref, act_ref = refs[18:23]
    acc_ref = refs[23] if natural else y_ref
    batch, size, width = x_ref.shape
    n = pl.program_id(0)

    @pl.when(n < first_steps)
    def _():
        high, low = split(wo_ref[0])
        put_right(ro_ref, high, low, 0)
        group = math.gcd(batch, 3)
        for g in range(0, batch, group):
            block = range(g, g + group)
            state = [eq_ref[b, 0:8] + eq_ref[b, 8:16] * inc_ref[b : b + 1] for b in block]
            for r in range(0, size, 16):
                for k, b in enumerate(block):
                    pair = []
                    for rows in (slice(r, r + 8), slice(r + 8, r + 16)):
                        gate = sg_ref[b, rows, :]
                        decay = (1.0 - gate) * m_ref[b, rows, 1:2]
                        state[k] = decay * state[k] + gate * sp_ref[b, rows, :]
                        pair.append(state[k])
                    rows = slice(b * size + r, b * size + r + 16)
                    sth_ref[rows, :], stl_ref[rows, :] = split(jnp.concatenate(pair, 0))
            for b in block:
                rows = slice(b * size, (b + 1) * size)
                left = jnp.concatenate([sth_ref[rows, :], stl_ref[rows, :], sth_ref[rows, :]], 1)
                mid_ref[b] = dot(left, ro_ref[...]) + jnp.where(n == 0, x_ref[b], mid_ref[b])

    @pl.when(n == first_steps)
    def _():
        gain = gain_ref[layer : layer + 1]

        def prepare(b, _):
            for r in range(0, size, 16):
                middle = mid_ref[b, r : r + 16, :]
                acc_ref[b, r : r + 16, :] = middle
                rows = pl.ds(pl.multiple_of(b * size + r, 16), 16)
                put_left(cat_ref, middle * inverse_rms(middle) * gain, rows)
            return _

        lax.fori_loop(0, batch, prepare, 0)

    @pl.when(n >= first_steps)
    def _():
        high, low = split(up_ref[0])
        put_right(ru_ref, high, low, 0)
        high, low = split(dn_ref[0])
        put_right(rd_ref, high, low, 0)

        def product(b):
            return dot(cat_ref[b * size : (b + 1) * size, :], ru_ref[...])

        ahead = product(0)
        for b in range(batch):
            now = ahead
            if b + 1 < batch:
                ahead = product(b + 1)
            act = act_ref.at[b % 2]
            for r in range(0, size, 16):
                pre = now[r : r + 16]
                pre_ref[b * size + r : b * size + r + 16, :] = pre
                put_left(act, pre * gelu_parts(pre)[2], slice(r, r + 16))
            turn_slice(cat_ref, b, size, n - first_steps, nth_ref, ntl_ref)
            acc_ref[b] += dot(act[...], rd_ref[...])

    @pl.when(n == pl.num_programs(0) - 1)
    def _():
        count = last_ref.shape[1]

        def finish(b, _):
            for k in range(count):
                row = size - 8 * (count - k) + 7
                last_ref[b, k : k + 1, :] = acc_ref[b, row : row + 1, :]
            if natural:
                store_rows(y_ref, b, lambda r: acc_ref[b, r : r + 8, :])
            return _

        lax.fori_loop(0, batch, finish, 0)


def emit(mine, tile, keep_ref, send_ref, plan, half=0):
    kind, depth, lanes, halves = plan
    if kind == "whole":
        keep_ref[half] = tile
        return
    extra = (0,) if halves == 1 else (half, 0)

    def store(core, ref):
        if kind == "plain":
            zs, ks = ref.shape[-4], ref.shape[-3]
            for z in range(zs):
                for k in range(ks):
                    top = (z * 2 + core) * depth
                    ref[extra + (z, k)] = tile[top : top + depth, 128 * k : 128 * (k + 1)]
        else:
            for r in range(ref.shape[0]):
                for z in range(ref.shape[1]):
                    for k in range(ref.shape[2]):
                        left = (z * 2 + core) * lanes + 128 * k
                        ref[r, z, k] = tile[r * depth : (r + 1) * depth, left : left + 128]

    def stores(core):
        store(core, keep_ref)
        store(1 - core, send_ref)

    pl.when(mine == 0)(lambda: stores(0))
    pl.when(mine != 0)(lambda: stores(1))


def three(high_ref, low_ref):
    return jnp.concatenate([high_ref[...], high_ref[...], low_ref[...]], 0)


def ffn_back_kernel(natural, layer, plans, afters, *refs):
    refs = refs[afters:]
    mine_ref, gy_ref, got_ref, last_ref, first_ref, mid_hbm, gain_ref, nth_hbm, ntl_hbm, pre_ref, dn_ref, up_ref = refs[:12]
    gm_ref, sec_ref, dk_ref, ds_ref, uk_ref, us_ref = refs[12:18]
    cat_ref, gyt_ref, ah_ref, al_ref, gh_ref, gl_ref, rd_ref, ru_ref, gn_ref = refs[18:27]
    mid_ref, nth_ref, ntl_ref, sems = refs[27:31]
    batch, size, width = gy_ref.shape
    n = pl.program_id(0)
    mine = mine_ref[0]
    gain = gain_ref[layer : layer + 1]
    pairs = ((nth_hbm, nth_ref), (ntl_hbm, ntl_ref), (mid_hbm, mid_ref))
    copies = [pltpu.make_async_copy(a, b, sems.at[k]) for k, (a, b) in enumerate(pairs)]

    @pl.when(n == 0)
    def _():
        for copy in copies:
            copy.start()

        def prepare(b, _):
            start = pl.multiple_of(b * size, size)

            def put(r, gy):
                gm_ref[b, r : r + 8, :] = gy

            load_rows(gy_ref, b, natural, put)
            if not natural:
                count = last_ref.shape[1]
                at = lax.broadcasted_iota(jnp.int32, (8, width), 0) == 7
                delta = norm_back(got_ref[b] * first_ref[layer + 1 : layer + 2], last_ref[b])
                for k in range(count):
                    row = size - 8 * (count - k)
                    gm_ref[b, row : row + 8, :] += jnp.where(at, delta[k : k + 1], 0.0)
            for r in range(0, size, 16):
                put_left(cat_ref, gm_ref[b, r : r + 16, :], pl.ds(pl.multiple_of(start + r, 16), 16))
            put_left_turned(gyt_ref, gm_ref[b], start)
            return _

        lax.fori_loop(0, batch, prepare, 0)
        sec_ref[...] = jnp.zeros_like(sec_ref)
        gn_ref[...] = jnp.zeros_like(gn_ref)

    high, low = split(dn_ref[0])
    put_right(rd_ref, high, low, 1)
    high, low = split(up_ref[0])
    put_right(ru_ref, high, low, 1)

    def product(b):
        return dot(cat_ref[b * size : (b + 1) * size, :], rd_ref[...], NT)

    ahead = product(0)
    for b in range(batch):
        now = ahead
        if b + 1 < batch:
            ahead = product(b + 1)
        for r in range(0, size, 16):
            rows = slice(b * size + r, b * size + r + 16)
            pre = pre_ref[rows, :]
            sq, tan, half = gelu_parts(pre)
            ah_ref[rows, :], al_ref[rows, :] = split(pre * half)
            slope = half + (0.5 * pre) * (1.0 - tan * tan) * (C0 + (3.0 * C1) * sq)
            gh_ref[rows, :], gl_ref[rows, :] = split(now[r : r + 16] * slope)
        rows = slice(b * size, (b + 1) * size)
        left = jnp.concatenate([gh_ref[rows, :], gl_ref[rows, :], gh_ref[rows, :]], 1)
        gn_ref[rows, :] += dot(left, ru_ref[...], NT)
    emit(mine, dot(gyt_ref[...], three(ah_ref, al_ref)), dk_ref, ds_ref, plans[0])

    @pl.when(n == 0)
    def _():
        copies[0].wait()
        copies[1].wait()

    emit(mine, dot(three_left(nth_ref, ntl_ref), three(gh_ref, gl_ref)), uk_ref, us_ref, plans[1])

    @pl.when(n == pl.num_programs(0) - 1)
    def _():
        copies[2].wait()

        def finish(b, _):
            total = sec_ref[...]
            for r in range(0, size, 16):
                gn = gn_ref[pl.ds(pl.multiple_of(b * size + r, 16), 16), :]
                middle = mid_ref[b, r : r + 16, :]
                scale = inverse_rms(middle)
                hat = middle * scale
                total = total + row_sum(gn * hat)
                gg = gn * gain
                mean = jnp.mean(gg * hat, -1, keepdims=True)
                gm_ref[b, r : r + 16, :] = gm_ref[b, r : r + 16, :] + scale * (gg - hat * mean)
            sec_ref[...] = total
            return _

        lax.fori_loop(0, batch, finish, 0)


def out_back_kernel(afters, *refs):
    gm_ref, m_ref, sg_ref, wo_ref, gs_ref, beq_ref, own_ref, gth_ref, gtl_ref, cat_ref, ro_ref = refs[afters:]
    batch, size, width = gm_ref.shape
    step = sg_ref.shape[-1]
    n = pl.program_id(0)

    def prepare(b):
        for r in range(0, size, 16):
            put_left(cat_ref, gm_ref[b, r : r + 16, :], slice(b * size + r, b * size + r + 16))

    def product(b):
        return dot(cat_ref[b * size : (b + 1) * size, :], ro_ref[...], NT)

    def body(first, _):
        if first:
            prepare(0)
        high, low = split(wo_ref[0])
        put_right(ro_ref, high, low, 1)
        ahead = product(0)
        for b in range(batch):
            gs_ref[b] = ahead
            if b + 1 < batch:
                if first:
                    prepare(b + 1)
                ahead = product(b + 1)
            local = jnp.zeros((8, step), F32)
            total = jnp.ones((8, step), F32)
            for i in reversed(range(size // 8)):
                rows = slice(i * 8, (i + 1) * 8)
                decay = (1.0 - sg_ref[b, rows, :]) * m_ref[b, rows, 1:2]
                local = decay * (gs_ref[b, rows, :] + local)
                total = decay * total
            turn_slice(cat_ref, b, size, n, gth_ref, gtl_ref)
            parts = chunk_scan(total, local, True)
            beq_ref[b, 0:8, :] = parts[0]
            beq_ref[b, 8:16, :] = parts[1]
            own_ref[0, b : b + 1, :] = parts[3][0:1]
            own_ref[1, b : b + 1, :] = parts[2][0:1]

    pl.when(n == 0)(lambda: body(True, False))
    pl.when(n != 0)(lambda: body(False, False))


def out_grad_kernel(plan, afters, *refs):
    mine_ref, gth_ref, gtl_ref, sth_ref, stl_ref = refs[afters : afters + 5]
    ok_ref, os_ref = refs[-2:]
    emit(mine_ref[0], dot(three_left(gth_ref, gtl_ref), three(sth_ref, stl_ref)), ok_ref, os_ref, plan)


def gates_back_kernel(plan, afters, *refs):
    refs = refs[afters:]
    mine_ref, gs_ref, sg_ref, sp_ref, sth_ref, stl_ref, m_ref, beq_ref, ret_ref, inc_ref = refs[:10]
    mth_ref, mtl_ref = refs[10:12]
    glh_ref, gll_ref, gch_ref, gcl_ref, bias_ref, ik_ref, is_ref = refs[12:19]
    batch, size, step = sg_ref.shape
    mine = mine_ref[0]
    top = lax.broadcasted_iota(jnp.int32, (8, step), 0) == 0
    bias_sum = jnp.zeros((8, step), F32)
    group = math.gcd(batch, 2)

    def states(b, r):
        rows = slice(b * size + r, b * size + r + 16)
        return sth_ref[rows, :].astype(F32) + stl_ref[rows, :].astype(F32)

    for g in range(0, batch, group):
        block = range(g, g + group)
        carry = [beq_ref[b, 0:8] + beq_ref[b, 8:16] * ret_ref[b : b + 1] for b in block]
        here = [states(b, size - 16) for b in block]
        wrap = [jnp.where(top, inc_ref[b : b + 1], pltpu.roll(here[k][8:], 1, 0)) for k, b in enumerate(block)]
        for r in reversed(range(0, size, 16)):
            for k, b in enumerate(block):
                below = states(b, r - 16) if r else None
                logits, cands = [], []
                for q in (8, 0):
                    rows = slice(r + q, r + q + 8)
                    prev = here[k][:8] if q else (below[8:] if r else wrap[k])
                    gate = sg_ref[b, rows, :]
                    soft = sp_ref[b, rows, :]
                    other = 1.0 - gate
                    adjoint = gs_ref[b, rows, :] + carry[k]
                    through = adjoint * m_ref[b, rows, 1:2]
                    carry[k] = other * through
                    glogit = gate * other * (adjoint * soft - through * prev)
                    bias_sum = bias_sum + glogit
                    logits.insert(0, glogit)
                    cands.insert(0, adjoint * gate * (1.0 - jnp.exp(-soft)))
                here[k] = below
                rows = slice(b * size + r, b * size + r + 16)
                glh_ref[rows, :], gll_ref[rows, :] = split(jnp.concatenate(logits, 0))
                gch_ref[rows, :], gcl_ref[rows, :] = split(jnp.concatenate(cands, 0))
    bias_ref[...] = bias_sum
    right = jnp.concatenate([three(glh_ref, gll_ref), three(gch_ref, gcl_ref)], 1)
    tile = dot(three_left(mth_ref, mtl_ref), right)
    for half in range(2):
        emit(mine, tile[:, half * step : (half + 1) * step], ik_ref, is_ref, plan, half)


def conv_back_kernel(natural, layer, batch, afters, *refs):
    refs = refs[afters:]
    glh_ref, gll_ref, gch_ref, gcl_ref, m_ref, x_ref, edge_ref, gm_ref, taps_ref, gain_ref, w_ref = refs[:11]
    gx_ref, send_ref, s_ref = refs[11:14]
    right_ref, acc_ref, ext_ref, out_ref = refs[14:18]
    _, size, width = x_ref.shape
    taps = taps_ref.shape[0]
    head = 8 * (taps - 1)
    n = pl.program_id(0)

    def product(slot):
        high = jnp.concatenate([glh_ref[...], gch_ref[...]], 1)
        low = jnp.concatenate([gll_ref[...], gcl_ref[...]], 1)
        acc_ref[slot] = dot(jnp.concatenate([high, low, high], 1), right_ref[...], NT)

    def finish(slot):
        b = n - 1
        last = lax.broadcasted_iota(jnp.int32, (8, width), 0) == 7
        gain = gain_ref[layer : layer + 1]
        scales = []
        for r in range(0, size, 8):
            x = x_ref[0, r : r + 8, :]
            scales.append(inverse_rms(x))
            ext_ref[head + r : head + r + 8, :] = x * scales[-1]
        edge = edge_ref[b]
        extend(ext_ref, edge * inverse_rms(edge))

        def scaled(j, r):
            return taps_ref[j : j + 1] * (m_ref[b, r : r + 8, j : j + 1] * acc_ref[slot, r : r + 8, :])

        sends = [None] * taps
        tails = {}
        for j in range(1, taps):
            for k in range(j):
                piece = scaled(j, 8 * k)
                tails[j, k] = jnp.where(last, 0.0, pltpu.roll(piece, 7, 0))
                sends[j - k] = piece if sends[j - k] is None else sends[j - k] + piece
        for k in range(1, taps):
            send_ref[b, taps - 1 - k : taps - k, :] = sends[k][0:1]
        sums = [s_ref[8 * j : 8 * (j + 1)] for j in range(taps)]
        for r in range(0, size, 8):
            gmixed = acc_ref[slot, r : r + 8, :]
            hat = ext_ref[head + r : head + r + 8, :]
            gn = taps_ref[0:1] * gmixed
            sums[0] = sums[0] + gmixed * hat
            for j in range(1, taps):
                at = head + r - 8 * j
                sums[j] = sums[j] + m_ref[b, r : r + 8, j : j + 1] * gmixed * ext_ref[at : at + 8, :]
                ahead = r + 8 * j
                gn = gn + (scaled(j, ahead) if ahead < size else tails[j, (ahead - size) // 8])
            gg = gn * gain
            mean = jnp.mean(gg * hat, -1, keepdims=True)
            gx = gm_ref[0, r : r + 8, :] + scales[r // 8] * (gg - hat * mean)
            if natural:
                out_ref[r : r + 8, :] = gx
            else:
                gx_ref[0, r : r + 8, :] = gx
        for j in range(taps):
            s_ref[8 * j : 8 * (j + 1)] = sums[j]
        if natural:
            store_rows(gx_ref, 0, lambda r: out_ref[r : r + 8, :])

    @pl.when(n == 0)
    def _():
        s_ref[...] = jnp.zeros_like(s_ref)
        high, low = split(w_ref[0])
        put_right(right_ref, high, low, 1)
        product(0)

    for odd in range(2):

        @pl.when((n > 0) & (n < batch) & (n % 2 == odd))
        def _():
            product(odd)
            finish(1 - odd)

    @pl.when(n == batch)
    def _():
        finish((batch - 1) % 2)


def add_kernel(count, afters, *refs):
    refs = refs[afters:]
    out_ref = refs[2 * count]
    start = 0
    for k in range(count):
        rows = refs[2 * k].shape[-2]
        out_ref[:, :, start : start + rows, :] = refs[2 * k][...] + refs[2 * k + 1][...]
        start += rows


def shape(*dims, dtype=F32):
    return jax.ShapeDtypeStruct(dims, dtype)


def fixed(array):
    zero = (0,) * len(array.shape)
    return (array, pl.BlockSpec(array.shape, lambda n: zero, pipeline_mode=pl.Buffered(1)))


def in_hbm(array):
    return (array, pl.BlockSpec(memory_space=pltpu.HBM))


def out_fixed(*dims):
    zero = (0,) * len(dims)
    return (shape(*dims), pl.BlockSpec(dims, lambda n: zero))


def chunked(array, at=lambda n: n, axis=-1, layer=None, step=CHUNK):
    dims = list(array.shape)
    axis = axis % len(dims)
    dims[axis] = step
    if layer is not None:
        dims[0] = 1

    def index(n):
        place = [0] * len(dims)
        place[axis] = at(n)
        if layer is not None:
            place[0] = layer
        return tuple(place)

    return (array, pl.BlockSpec(tuple(dims), index))


def block_bytes(dims, dtype):
    dims = [1 if d is None else d for d in dims]
    size = jnp.dtype(dtype).itemsize
    dims[-1] = -(-dims[-1] // 128) * 128
    if len(dims) > 1:
        dims[-2] = -(-dims[-2] // 8) * 8
    return math.prod(dims) * size


def vmem_need(ins, outs, scratch):
    total = 8 * 1024 * 1024
    for array, spec in list(ins) + list(outs):
        if spec.block_shape is not None:
            total += block_bytes(spec.block_shape, array.dtype) * (2 if spec.pipeline_mode is None else 1)
    for ref in scratch:
        if ref.memory_space == pltpu.VMEM:
            total += block_bytes(ref.shape, ref.dtype)
    return min(total, VMEM)


def call(kernel, grid, ins, outs, scratch=(), flops=0, name=None, free=False, aliases=()):
    def large(array):
        return math.prod(array.shape) * array.dtype.itemsize > LARGE

    args = [
        pltpu.with_memory_space_constraint(array, pltpu.HBM)
        if spec.memory_space == pltpu.HBM or (spec.memory_space is None and large(array) and not free)
        else array
        for array, spec in ins
    ]
    shapes = [pltpu.HBM(array.shape, array.dtype) if large(array) and not free else array for array, _ in outs]
    moved = sum(math.prod(a.shape) * a.dtype.itemsize for a, _ in ins)
    moved += sum(math.prod(a.shape) * a.dtype.itemsize for a, _ in outs)
    return pl.pallas_call(
        kernel,
        grid=(grid,),
        in_specs=[s for _, s in ins],
        out_specs=[s for _, s in outs],
        out_shape=shapes,
        scratch_shapes=list(scratch),
        compiler_params=pltpu.CompilerParams(
            vmem_limit_bytes=vmem_need(ins, outs, scratch), dimension_semantics=("arbitrary",)
        ),
        cost_estimate=pl.CostEstimate(flops=int(flops), bytes_accessed=int(moved), transcendentals=0),
        name=name,
        input_output_aliases=dict(aliases),
    )(*args)


def kept_back(arrays):
    return [in_hbm(a) for a in arrays]


def shift(block, distance):
    size = lax.axis_size("seq")
    route = [(i - distance, i) for i in range(size) if 0 <= i - distance < size]
    return lax.ppermute(block, "seq", route)


def partner(block, flip):
    return lax.ppermute(block, "seq", [(i, i ^ flip) for i in range(lax.axis_size("seq"))])


def combine(earlier, later):
    return jnp.stack([earlier[0] * later[0], later[0] * earlier[1] + later[1]])


def carry_kernel(afters, flag_ref, first_ref, second_ref, out_ref):
    swap = flag_ref[0] == 0
    first, second = first_ref[...], second_ref[...]
    earlier = jnp.where(swap, second, first)
    later = jnp.where(swap, first, second)
    out_ref[0] = earlier[0] * later[0]
    out_ref[1] = later[0] * earlier[1] + later[1]


def joined_carry(first, second, flag, afters):
    def kernel(*refs):
        carry_kernel(0, *refs[len(afters) :])

    flag = (flag.astype(jnp.int32).reshape(1), pl.BlockSpec(memory_space=pltpu.SMEM))
    return call(
        kernel,
        1,
        kept_back(afters) + [flag, fixed(first), fixed(second)],
        [out_fixed(*first.shape)],
        name="carry",
    )[0]


def incoming_carry(own, back, fillers=((), ())):
    size = lax.axis_size("seq")
    other = partner(own, 1)
    odd = lax.axis_index("seq") % 2 == 1
    is_later = ~odd if back else odd
    if back:
        pair = joined_carry(other, own, is_later, fillers[0])
    else:
        pair = jnp.where(is_later, combine(other, own), combine(own, other))
    sign = -2 if back else 2
    before = None
    dist = 1
    while dist < size // 2:
        got = shift(pair, sign * dist)
        before = got if before is None else combine(got, before)
        if 2 * dist < size // 2:
            if back and dist == 1:
                pair = joined_carry(got, pair, jnp.ones((), jnp.int32), fillers[1])
            else:
                pair = combine(got, pair)
        dist *= 2
    if back:
        return functools.partial(entering_carry, is_later, other, before), pair
    return jnp.where(is_later, other[0] * before[1] + other[1], before[1])


def entering_carry(is_later, other, before, afters):
    def kernel(*refs):
        flag, other_ref, before_ref, out_ref = refs[len(afters) :]
        further = other_ref[0] * before_ref[1] + other_ref[1]
        out_ref[...] = jnp.where(flag[0] != 0, further, before_ref[1])

    flag = (is_later.astype(jnp.int32).reshape(1), pl.BlockSpec(memory_space=pltpu.SMEM))
    return call(
        kernel,
        1,
        kept_back(afters) + [flag, fixed(other), fixed(before)],
        [out_fixed(*other.shape[1:])],
        name="carry",
    )[0]


def document_masks(starts_rows, group):
    place = jnp.arange(group, dtype=jnp.int32)
    position = lax.axis_index("seq") * group + (place % 8) * (group // 8) + place // 8
    back = position[:, None] - jnp.arange(8, dtype=jnp.int32)

    def document(at):
        return sum((starts_rows[:, k, None, None] <= at).astype(jnp.int32) for k in range(starts_rows.shape[1]))

    return (document(back) == document(position[:, None])).astype(F32)


class Grad:
    def __init__(self, height, width, flip, direct, step, halves=1):
        self.rows = lax.axis_size("rows")
        self.seq = lax.axis_size("seq")
        self.flip = flip
        self.direct = direct
        self.height = height
        self.width = width
        self.depth = height // (self.rows if flip else self.seq)
        self.lanes = width * halves // (self.seq if flip else self.rows)
        zs = self.seq // 2
        if not direct:
            self.plan = ("whole", 0, 0, halves)
            self.out = (shape(halves, height, width), pl.BlockSpec((halves, height, step), lambda n: (0, 0, n)))
        elif flip:
            self.plan = ("flip", self.depth, self.lanes, 1)
            ks = self.lanes // 128
            dims = (self.rows, zs, ks, self.depth, 128)
            block = (self.rows, step // (2 * self.lanes), ks, self.depth, 128)
            self.out = (shape(*dims), pl.BlockSpec(block, lambda n: (0, n, 0, 0, 0)))
        else:
            self.plan = ("plain", self.depth, self.lanes, halves)
            per = self.lanes // step
            dims = (self.rows // halves, zs, self.lanes // 128, self.depth, 128)
            block = (1, zs, step // 128, self.depth, 128)
            if halves == 1:
                self.out = (shape(*dims), pl.BlockSpec(block, lambda n: (n // per, 0, n % per, 0, 0)))
            else:
                spec = pl.BlockSpec((halves,) + block, lambda n: (0, n // per, 0, n % per, 0, 0))
                self.out = (shape(halves, *dims), spec)

    def outs(self, at=lambda n: n):
        array, spec = self.out
        out = (array, pl.BlockSpec(spec.block_shape, lambda n: spec.index_map(at(n))))
        return [out, out if self.direct else out_fixed(8, 128)]

    def pieces(self, array):
        return array.reshape(self.rows, self.seq // 2, -1, 128)

    def whole(self, array):
        out = array.reshape(self.lanes // 128, self.depth, 128).swapaxes(0, 1).reshape(self.depth, self.lanes)
        return out.T if self.flip else out

    def plain_sum(self, value):
        value = jnp.concatenate(list(value), 1)
        value = lax.psum_scatter(value, "seq", scatter_dimension=1 if self.flip else 0, tiled=True)
        value = lax.psum_scatter(value, "rows", scatter_dimension=0 if self.flip else 1, tiled=True)
        return value.T if self.flip else value


def butterfly(value):
    for axis in ("seq", "rows"):
        size = lax.axis_size(axis)
        flip = 1
        while flip < size:
            value = value + lax.ppermute(value, axis, [(i, i ^ flip) for i in range(size)])
            flip *= 2
    return value


def pack_small(smalls, taps, afters):
    layers = len(smalls)
    width = smalls[0][0].shape[1]
    hidden = smalls[0][2].shape[1]
    count = hidden // width

    def kernel(*refs):
        refs = refs[len(afters) :]
        out_ref = refs[-1]
        for layer in range(layers):
            sums, sec, bias = refs[3 * layer : 3 * layer + 3]
            for j in range(taps):
                out_ref[layer, j : j + 1, :] = jnp.sum(sums[8 * j : 8 * (j + 1)], 0, keepdims=True)
            out_ref[layer, taps : taps + 1, :] = jnp.sum(sec[...], 0, keepdims=True)
            for k in range(count):
                row = jnp.sum(bias[:, k * width : (k + 1) * width], 0, keepdims=True)
                out_ref[layer, taps + 1 + k : taps + 2 + k, :] = row

    return call(
        kernel,
        1,
        kept_back(afters) + [fixed(a) for group in smalls for a in group],
        [out_fixed(layers, taps + 1 + count, width)],
        name="pack_small",
        free=True,
    )[0]


def pair_sum(parts, afters=()):
    ins = []
    for kept, sent in parts:
        got = partner(sent, 1)
        ins += [kept, got]
    count = len(parts)
    rows, zs = ins[0].shape[:2]
    total = sum(a.shape[2] for a in ins[::2])
    return call(
        functools.partial(add_kernel, count, len(afters)),
        rows,
        kept_back(afters)
        + [(a, pl.BlockSpec((1,) + a.shape[1:], lambda n: (n, 0, 0, 0))) for a in ins],
        [(shape(rows, zs, total, 128), pl.BlockSpec((1, zs, total, 128), lambda n: (n, 0, 0, 0)))],
        name="neighbour_sum",
        free=True,
    )[0]


def reduce_rows(pieces):
    return lax.psum_scatter(pieces, "rows", scatter_dimension=0, tiled=True)[0]


def seq_step(arrays, dist, got=None, afters=()):
    count = len(arrays)
    places = arrays[0].shape[0]
    total = sum(a.shape[1] for a in arrays)
    bit = ((lax.axis_index("seq") // 2 // dist) % 2).astype(jnp.int32).reshape(1)

    def kernel(*refs):
        refs = refs[len(afters) :]
        own = refs[0][0]
        ins = refs[1 : 1 + count]
        more = refs[1 + count] if got is not None else None
        outs = refs[1 + count + (got is not None) :]
        start = 0
        for ref in ins:
            rows = ref.shape[1]
            for z in range(places):
                value = ref[z]
                if more is not None:
                    value = value + more[z, start : start + rows, :]
                if places == 1:
                    outs[0][0, start : start + rows, :] = value
                    continue

                def put(ref, value=value, start=start, rows=rows, z=z):
                    ref[z // 2, start : start + rows, :] = value

                pl.when(own == z % 2)(functools.partial(put, outs[0]))
                pl.when(own != z % 2)(functools.partial(put, outs[1]))
            start += rows

    half = max(1, places // 2)
    return call(
        kernel,
        1,
        kept_back(afters)
        + [(bit, pl.BlockSpec(memory_space=pltpu.SMEM))]
        + [fixed(a) for a in arrays]
        + ([fixed(got)] if got is not None else []),
        [out_fixed(half, total, 128) for _ in range(2 if places > 1 else 1)],
        name="seq_sum",
    )


def reduce_seq(kept, afters=()):
    dist = 1
    while len(kept) == 2:
        got = partner(kept[1], 2 * dist)
        dist *= 2
        kept = seq_step([kept[0]], dist, got, afters)
    return kept[0][0]


def per_device(
    inputs,
    starts,
    first_gain,
    conv_taps,
    in_weight,
    gate_bias,
    out_weight,
    second_gain,
    up_weight,
    down_weight,
    cotangent,
):
    dims = inputs.shape
    batch = dims[0] * dims[1]
    group = dims[2]
    width = dims[3]
    tokens = batch * group
    taps = conv_taps.shape[2]
    layers = in_weight.shape[0]
    hidden = out_weight.shape[1]
    ff = up_weight.shape[2]
    rows_size, seq_size = lax.axis_size("rows"), lax.axis_size("seq")
    direct = (
        ff % (CHUNK * rows_size) == 0
        and (2 * hidden) % (HALF * rows_size) == 0
        and rows_size % 2 == 0
        and all(n % (128 * seq_size) == 0 and CHUNK % (2 * n // seq_size) == 0 for n in (ff, hidden))
    )
    extended = pltpu.VMEM((8 * (taps - 1) + group, width), F32)
    mine = (lax.axis_index("seq") % 2).astype(jnp.int32).reshape(1)
    mine = (mine, pl.BlockSpec(memory_space=pltpu.SMEM))
    masks = document_masks(starts.reshape(batch, -1), group)
    taps_rows = conv_taps.swapaxes(1, 2)
    in_flops = 6 * tokens * width * 2 * hidden
    out_flops = 6 * tokens * width * hidden
    ffn_flops = 6 * tokens * width * ff * 2

    current = inputs.reshape(batch, group, width)
    last_rows = current[:, group - taps + 1 :]
    row_hidden = shape(batch, group, hidden)
    row_eq = shape(batch, 16, hidden)
    row_own = shape(2, batch, hidden)
    turned = shape(width, tokens, dtype=BF)
    saved = []
    for layer in range(layers):
        natural = layer == 0
        final = layer == layers - 1
        edge = shift(last_rows, 1)
        steps = hidden // CHUNK
        res = call(
            functools.partial(gates_kernel, natural, layer),
            steps,
            [fixed(current), fixed(edge), fixed(masks), fixed(first_gain), fixed(taps_rows[layer])]
            + [chunked(in_weight, layer=layer), chunked(in_weight, lambda n: n + steps, layer=layer)]
            + [chunked(gate_bias)],
            [chunked(row_hidden), chunked(row_hidden), chunked(row_eq), chunked(row_own)]
            + [chunked(turned, axis=0, step=width // steps) for _ in range(2)]
            + ([out_fixed(batch, group, width)] if natural else []),
            scratch=[pltpu.VMEM((tokens, 3 * width), BF), pltpu.VMEM((3 * width, 2 * CHUNK), BF), extended],
            flops=in_flops,
            name="gates",
        )
        sg, sp, eq, own = res[:4]
        mixt = res[4:6]
        x = res[6] if natural else current
        inc = incoming_carry(own, False)
        early_steps = hidden // HALF

        def early(n):
            return jnp.minimum(n, early_steps - 1)

        def late(n):
            return jnp.maximum(n - early_steps, 0)

        def halves(array):
            return chunked(array, early, step=HALF)

        res = call(
            functools.partial(ffn_kernel, final, layer, early_steps),
            early_steps + ff // CHUNK,
            [fixed(x), fixed(masks), halves(sg), halves(sp), halves(eq), halves(inc)]
            + [chunked(out_weight, early, axis=1, layer=layer, step=HALF), fixed(second_gain)]
            + [chunked(up_weight, late, layer=layer), chunked(down_weight, late, axis=1, layer=layer)],
            [
                out_fixed(batch, group, width),
                out_fixed(batch, taps - 1, width),
                out_fixed(batch, group, width),
                halves(shape(tokens, hidden, dtype=BF)),
                halves(shape(tokens, hidden, dtype=BF)),
                chunked(shape(tokens, ff), late),
                chunked(turned, late, axis=0, step=width // (ff // CHUNK)),
                chunked(turned, late, axis=0, step=width // (ff // CHUNK)),
            ],
            scratch=[
                pltpu.VMEM((tokens, 3 * width), BF),
                pltpu.VMEM((3 * HALF, width), BF),
                pltpu.VMEM((3 * width, CHUNK), BF),
                pltpu.VMEM((3 * CHUNK, width), BF),
                pltpu.VMEM((2, group, 3 * CHUNK), BF),
            ]
            + ([pltpu.VMEM((batch, group, width), F32)] if final else []),
            flops=out_flops + ffn_flops,
            name="ffn",
        )
        current, following, mid, st, pre, nt = res[0], res[1], res[2], res[3:5], res[5], res[6:8]
        saved.append((x, last_rows, edge, sg, sp, inc, mid, st, pre, mixt, nt))
        last_rows = following
    outputs = current

    grad = cotangent.reshape(batch, group, width)
    got = jnp.zeros((batch, taps - 1, width), F32)
    down_plan = Grad(width, ff, True, direct, CHUNK)
    up_plan = Grad(width, ff, False, direct, CHUNK)
    out_plan = Grad(width, hidden, True, direct, CHUNK)
    in_plan = Grad(width, hidden, False, direct, HALF, 2)
    shards = [None] * layers
    smalls = [None] * layers
    early_rows = [None] * layers
    late_rows = [None] * layers
    for layer in reversed(range(layers)):
        x, last_rows, edge, sg, sp, inc, mid, st, pre, mixt, nt = saved[layer]
        final = layer == layers - 1
        first = layer == 0
        above = last_rows if final else saved[layer + 1][1]
        waiting = [early_rows[layer + 1]] if direct and not final else []
        res = call(
            functools.partial(ffn_back_kernel, final, layer, (down_plan.plan, up_plan.plan), len(waiting)),
            ff // CHUNK,
            kept_back(waiting)
            + [mine, fixed(grad), fixed(got), fixed(above), fixed(first_gain)]
            + [in_hbm(mid), fixed(second_gain), in_hbm(nt[0]), in_hbm(nt[1]), chunked(pre)]
            + [chunked(down_weight, axis=1, layer=layer), chunked(up_weight, layer=layer)],
            [out_fixed(batch, group, width), out_fixed(8, width)] + down_plan.outs() + up_plan.outs(),
            scratch=[
                pltpu.VMEM((tokens, 3 * width), BF),
                pltpu.VMEM((width, 3 * tokens), BF),
                pltpu.VMEM((tokens, CHUNK), BF),
                pltpu.VMEM((tokens, CHUNK), BF),
                pltpu.VMEM((tokens, CHUNK), BF),
                pltpu.VMEM((tokens, CHUNK), BF),
                pltpu.VMEM((CHUNK, 3 * width), BF),
                pltpu.VMEM((width, 3 * CHUNK), BF),
                pltpu.VMEM((tokens, width), F32),
                pltpu.VMEM((batch, group, width), F32),
                pltpu.VMEM((width, tokens), BF),
                pltpu.VMEM((width, tokens), BF),
                pltpu.SemaphoreType.DMA((3,)),
            ],
            flops=2 * ffn_flops,
            name="ffn_back",
        )
        gm, sec, down_g, up_g = res[0], res[1], res[2:4], res[4:6]
        waiting = []
        if direct and not final:
            z_next = seq_step([early_rows[layer + 1], late_rows[layer + 1]], 1, None, [gm])
            waiting = [z_next[1]]
        res = call(
            functools.partial(out_back_kernel, len(waiting)),
            hidden // CHUNK,
            kept_back(waiting) + [fixed(gm), fixed(masks), chunked(sg), chunked(out_weight, axis=1, layer=layer)],
            [chunked(row_hidden), chunked(row_eq), chunked(row_own)]
            + [chunked(turned, axis=0, step=width // (hidden // CHUNK)) for _ in range(2)],
            scratch=[pltpu.VMEM((tokens, 3 * width), BF), pltpu.VMEM((CHUNK, 3 * width), BF)],
            flops=out_flops,
            name="out_back",
        )
        gs, beq, own, gmt = res[0], res[1], res[2], res[3:5]

        def out_grad(chunk, before, afters):
            def place(n):
                return chunk

            ins = kept_back(afters) + [mine, fixed(gmt[0]), fixed(gmt[1]), chunked(st[0], place), chunked(st[1], place)]
            outs = out_plan.outs(place)
            return call(
                functools.partial(out_grad_kernel, out_plan.plan, len(afters)),
                1,
                ins + kept_back(before),
                outs,
                flops=out_flops * CHUNK // hidden,
                name="out_grad",
                aliases=[(len(ins) + k, k) for k in range(len(before))],
            )

        out_g = out_grad(0, (), ())
        waiting = []
        fillers = [[], [out_g[0]]]
        if direct:
            early_parts = [tuple(down_plan.pieces(v) for v in down_g), tuple(up_plan.pieces(v) for v in up_g)]
            if first:
                early = pair_sum(early_parts, [gs])
                early_rows[layer] = reduce_rows(early)
                fillers[0].append(early)
        enters, last_pair = incoming_carry(own, True, fillers)
        for chunk in range(1, hidden // CHUNK):
            out_g = out_grad(chunk, out_g, [last_pair])
        ret = enters([out_g[0]])
        if direct and not first:
            early = pair_sum(early_parts, [last_pair])
            early_rows[layer] = reduce_rows(early)
            waiting.append(early)
        if direct and not final:
            z_next = seq_step([z_next[0]], 2, partner(z_next[1], 2), [last_pair])
            waiting.append(z_next[-1])
        steps = hidden // HALF
        halves = functools.partial(chunked, step=HALF)
        res = call(
            functools.partial(gates_back_kernel, in_plan.plan, len(waiting)),
            steps,
            kept_back(waiting)
            + [mine, halves(gs), halves(sg), halves(sp), halves(st[0]), halves(st[1]), fixed(masks)]
            + [halves(beq), halves(ret), halves(inc)]
            + [fixed(mixt[0]), fixed(mixt[1])],
            [halves(shape(tokens, hidden, dtype=BF)) for _ in range(4)] + [halves(shape(8, hidden))] + in_plan.outs(),
            flops=in_flops,
            name="gates_back",
        )
        gproj, bias_sum, in_g = res[:4], res[4], res[5:7]
        waiting = []
        late_parts = None
        if direct:
            late_parts = [tuple(out_plan.pieces(v) for v in out_g), tuple(in_plan.pieces(v) for v in in_g)]
            if first:
                halved = seq_step([early_rows[layer]], 1, None, [bias_sum])
                late = pair_sum(late_parts, [halved[-1]])
                late_rows[layer] = reduce_rows(late)
                waiting = [late]

        def now(n):
            return jnp.minimum(n, batch - 1)

        def lag(n):
            return jnp.maximum(n - 1, 0)

        res = call(
            functools.partial(conv_back_kernel, first, layer, batch, len(waiting)),
            batch + 1,
            kept_back(waiting)
            + [chunked(g, now, axis=0, step=group) for g in gproj]
            + [fixed(masks), chunked(x, lag, axis=0, step=1), fixed(edge), chunked(gm, lag, axis=0, step=1)]
            + [fixed(taps_rows[layer]), fixed(first_gain)]
            + [(in_weight, pl.BlockSpec((1, width, 2 * hidden), lambda n: (layer, 0, 0), pipeline_mode=pl.Buffered(1)))],
            [
                chunked(shape(batch, group, width), lag, axis=0, step=1),
                out_fixed(batch, taps - 1, width),
                out_fixed(8 * taps, width),
            ],
            scratch=[pltpu.VMEM((width, 6 * hidden), BF), pltpu.VMEM((2, group, width), F32)]
            + [extended, pltpu.VMEM((group, width), F32)],
            flops=in_flops,
            name="conv_back",
        )
        grad, send, sums = res
        if direct and not first:
            late_rows[layer] = reduce_rows(pair_sum(late_parts, [grad]))
        if not direct:
            shards[layer] = (
                in_plan.plain_sum(in_g[0]),
                out_plan.plain_sum(out_g[0]),
                up_plan.plain_sum(up_g[0]),
                down_plan.plain_sum(down_g[0]),
            )
        got = shift(send, -1)
        if first:
            grad = grad.at[:, group - taps + 1 :].add(norm_back(got * first_gain[layer], last_rows))
        smalls[layer] = (sums, sec, bias_sum)

    if direct:
        down_k = down_plan.depth * down_plan.lanes // 128
        up_k = up_plan.depth * up_plan.lanes // 128
        out_k = out_plan.depth * out_plan.lanes // 128
        above = seq_step([z_next[0]], 4, partner(z_next[1], 4), [sums])[0][0]
        halved = seq_step([halved[0]], 2, partner(halved[1], 2), [sums])
        packed = pack_small(smalls, taps, [])
        early = seq_step([halved[0]], 4, partner(halved[1], 4))[0][0]
        late = reduce_seq(seq_step([late_rows[0]], 1))
        done = [jnp.concatenate([early, late], 0), above]
        for layer in range(layers):
            parts = jnp.split(done[layer], [down_k, down_k + up_k, down_k + up_k + out_k])
            plans = (down_plan, up_plan, out_plan, in_plan)
            shards[layer] = tuple(plan.whole(part) for plan, part in zip(plans, parts))[::-1]
    else:
        packed = pack_small(smalls, taps, [])
    in_grad, out_grad, up_grad, down_grad = (jnp.stack([s[k] for s in shards]) for k in range(4))
    every = butterfly(packed)
    sums = every[:, :taps]
    first_grad = jnp.sum(sums * taps_rows, 1)
    taps_grad = (sums * first_gain[:, None]).swapaxes(1, 2)
    second_grad = every[:, taps]
    bias_grad = every[:, taps + 1 :].reshape(layers, hidden)
    return (
        outputs.reshape(dims),
        grad.reshape(dims),
        first_grad,
        taps_grad,
        in_grad,
        bias_grad,
        out_grad,
        second_grad,
        up_grad,
        down_grad,
    )


def solution(mesh):
    in_specs = (
        P(None, "rows", "seq", None),
        P(None, "rows", None),
        P(),
        P(),
        P(),
        P(),
        P(),
        P(),
        P(),
        P(),
        P(None, "rows", "seq", None),
    )
    out_specs = (
        P(None, "rows", "seq", None),
        P(None, "rows", "seq", None),
        P(),
        P(),
        P(None, "seq", "rows"),
        P(),
        P(None, "seq", "rows"),
        P(),
        P(None, "seq", "rows"),
        P(None, "seq", "rows"),
    )
    return jax.shard_map(
        per_device, mesh=mesh, in_specs=in_specs, out_specs=out_specs, check_vma=False
    )
```
